256 devices in a mesh: span: 16 (over z_lo, y, core), seq: 16 (over x, z_hi).
Axes of the slice: x: 4, y: 4, z: 8 (z_hi: 4, z_lo: 2; z = z_hi * 2 + z_lo), core: 2. Of those that a mesh axis runs over, the one named last changes fastest.
Arguments:
- qkv: bfloat16 [3, 16, 1024, 2048], P(None, 'span', 'seq'), may hold values from -6 to 6
- lengths: int32 [16], replicated, may hold values from 512 to 1024, as said below
Outputs:
- attended: bfloat16 [16, 1024, 2048], P('span', 'seq')
The draws below stay inside these ranges and needn't reach their ends.
Inputs may be any that keep to these rules, and one draw needn't show every extreme that they name: `lengths`: the live tokens of a span are its first ones; some span is full.
All inputs are finite; a program needn't handle non-finite values.
Results may differ from the reference program's by a relative error of at most 0.0065.
Values may be sent and summed in bfloat16 or wider, within the bound.
No kernel may reach another device: no remote copies, remote signals or barrier semaphores. Data moves between devices by JAX's collectives and lax.ppermute only.
A program may use at most 64 MiB of HBM per device.

```python
import jax
import jax.numpy as jnp
from jax import lax

HEADS = 16
HD = 128
TOKC = 1024
SPANS = 16


def draw_qkv(key, part):
    feature_count = HEADS * HD
    shape = (3, SPANS, TOKC, feature_count)
    fields = jnp.clip(jax.random.normal(jax.random.fold_in(key, 12), shape, jnp.float32), -6.0, 6.0)
    return fields.astype(jnp.bfloat16)


def draw_lengths(key, part):
    drawn = jax.random.randint(jax.random.fold_in(key, 5), (SPANS,), TOKC // 2, TOKC + 1)
    full_span = jax.random.randint(jax.random.fold_in(key, 6), (), 0, SPANS)
    return jnp.where(jnp.arange(SPANS) == full_span, TOKC, drawn).astype(jnp.int32)


def setup_inputs(seed: int = 0) -> dict:
    keys = jax.random.split(jax.random.key(seed), 3)
    qkv = draw_qkv(jax.random.fold_in(keys[2], 71), 0)
    lengths = draw_lengths(jax.random.fold_in(keys[2], 71), 0)
    return {"qkv": qkv, "lengths": lengths}


masked_fill = -1e30


def block_terms(queries, key_rows, values, key_live):
    scores = jnp.einsum("hqe,hke->hqk", queries.astype(jnp.float32), key_rows.astype(jnp.float32)) * (key_rows.shape[-1] ** -0.5)
    scores = jnp.where(key_live[None, None, :], scores, masked_fill)
    row_peak = jnp.max(scores, axis=-1)
    weights = jnp.where(key_live[None, None, :], jnp.exp(scores - row_peak[..., None]), 0.0).astype(jnp.bfloat16)
    numerator = jnp.einsum("hqk,hke->hqe", weights.astype(jnp.float32), values.astype(jnp.float32))
    weight_sum = jnp.sum(weights.astype(jnp.float32), axis=-1)
    return row_peak, numerator, weight_sum


def combine(first_terms, second_terms):
    row_peak = jnp.maximum(first_terms[0], second_terms[0])
    scale_first = jnp.exp(first_terms[0] - row_peak)
    scale_second = jnp.exp(second_terms[0] - row_peak)
    numerator = first_terms[1] * scale_first[..., None] + second_terms[1] * scale_second[..., None]
    weight_sum = first_terms[2] * scale_first + second_terms[2] * scale_second
    return row_peak, numerator, weight_sum


def reference(qkv, lengths):
    positions = jnp.arange(TOKC)

    def split_heads(rows):
        return rows.reshape(TOKC, HEADS, HD).transpose(1, 0, 2)

    def per_span(span_index):
        queries = split_heads(qkv[0, span_index])
        initial = (jnp.full((HEADS, TOKC), masked_fill, jnp.float32), jnp.zeros((HEADS, TOKC, HD), jnp.float32), jnp.zeros((HEADS, TOKC), jnp.float32))

        def add_block(running, other_index):
            key_rows = split_heads(qkv[1, other_index])
            values = split_heads(qkv[2, other_index])
            key_live = (other_index <= span_index) & (positions < lengths[other_index])
            return combine(running, block_terms(queries, key_rows, values, key_live)), None

        final_terms, unused = lax.scan(add_block, initial, jnp.arange(SPANS))
        attended = final_terms[1] / final_terms[2][..., None]
        attended = attended.transpose(1, 0, 2).reshape(TOKC, HEADS * HD)
        return jnp.where((positions < lengths[span_index])[:, None], attended, 0.0).astype(jnp.bfloat16)

    return lax.map(per_span, jnp.arange(SPANS))
```

```python
import functools
import math

import jax
import jax.numpy as jnp
from jax import lax
from jax.experimental import pallas as pl
from jax.experimental.pallas import tpu as pltpu
from jax.sharding import Mesh
from jax.sharding import PartitionSpec as P

HD = 128
SLICE = 64
ROWS = 256
FILL = -1e30
EXTRA = 16
STATE = HD + EXTRA
SCALE = math.log2(math.e) / math.sqrt(HD)
VMEM = pltpu.VMEM
RING = ("zlo", "zhi")


def pack(qkv_ref, pair_ref, query_ref):
    for head in range(query_ref.shape[0]):
        columns = slice(head * HD, (head + 1) * HD)
        query_ref[head] = qkv_ref[0, :, columns]
        pair_ref[head, :SLICE] = qkv_ref[1, :, columns]
        pair_ref[head, SLICE:] = qkv_ref[2, :, columns]


def unpack(parts_ref, out_ref):
    for head in range(parts_ref.shape[0]):
        out_ref[:, head * HD : (head + 1) * HD] = parts_ref[head]


def attend(sources, first, *refs):
    refs = list(refs)
    lengths_ref, own_ref, other_ref = refs[:3]
    arrivals = refs[3 : 3 + len(sources)]
    before_ref = None if first else refs[3 + len(sources)]
    state_ref, turned_ref = refs[-2:]
    core = lax.axis_index("core")
    zlo = lax.axis_index("zlo")
    zed = lax.axis_index("zhi") * 2 + zlo
    chunks = []
    for number, (distance, begin) in enumerate(sources):
        for place in range(arrivals[number].shape[0] // 4):
            chunks.append((place + begin, number, place))
    chunks.sort()
    per_span = {}
    for span, number, place in chunks:
        per_span.setdefault(span, []).append((number, place))
    spans = sorted(per_span)
    source_zed = [lax.rem(zed + 8 + distance, 8) for distance, _ in sources]
    source_zlo = lax.rem(source_zed[0], 2)

    if first:
        state_ref[:, :, :HD + 8] = jnp.zeros_like(state_ref[:, :, :HD + 8])
        state_ref[:, :, HD + 8:] = jnp.full_like(state_ref[:, :, HD + 8:], FILL)
    else:
        state_ref[...] = before_ref[...]

    @pl.when(source_zlo <= zlo)
    def _():
        column = 0
        starts = []
        extra = jnp.where(lax.broadcasted_iota(jnp.int32, (EXTRA, ROWS), 0) < 8, 1.0, 0.0)
        for span in spans:
            starts.append(column)
            for number, place in per_span[span]:
                values = arrivals[number][4 * place : 4 * place + 4, SLICE:, :].reshape(ROWS, HD)
                turned_ref[:HD, column : column + ROWS] = values.T
                turned_ref[HD:, column : column + ROWS] = extra.astype(jnp.bfloat16)
                column += ROWS
        starts.append(column)

        def add(block_ref, rel, step, count):
            width = starts[count]
            queries = block_ref[step]
            scores = []
            for span in spans[:count]:
                live = lengths_ref[source_zlo * 8 + 2 * span + core]
                for number, place in per_span[span]:
                    keys = arrivals[number][4 * place : 4 * place + 4, :SLICE, :].reshape(ROWS, HD)
                    score = lax.dot_general(
                        keys, queries, (((1,), (1,)), ((), ())), preferred_element_type=jnp.float32
                    )
                    offset = (source_zed[number] // 2) * SLICE
                    row = lax.broadcasted_iota(jnp.int32, (SLICE, ROWS), 0)
                    pieces = [score[: 2 * SLICE]]
                    for piece in (2, 3):
                        bound = live - piece * ROWS - offset
                        part = score[piece * SLICE : (piece + 1) * SLICE]
                        pieces.append(jnp.where(row < bound, part, FILL))
                    scores.append(jnp.concatenate(pieces, axis=0))
            scores = jnp.concatenate(scores, axis=0)
            old_peak = state_ref[rel, step, HD + 8 : HD + 9, :]
            peak = jnp.maximum(old_peak, jnp.max(scores, axis=0, keepdims=True))
            weights = jnp.exp2((scores - peak) * SCALE).astype(jnp.bfloat16)
            fresh = jnp.dot(turned_ref[:, :width], weights, preferred_element_type=jnp.float32)
            keep = jnp.exp2((old_peak - peak) * SCALE)
            state_ref[rel, step, : HD + 8, :] = (
                state_ref[rel, step, : HD + 8, :] * keep + fresh[: HD + 8]
            )
            state_ref[rel, step, HD + 8 :, :] = jnp.broadcast_to(peak, (8, ROWS))

        for rel, block_ref in ((0, own_ref), (1, other_ref)):

            @pl.loop(0, 4)
            def _(step):
                mine = 2 * step + (core if rel == 0 else 1 - core)
                reach = jnp.where(source_zlo < zlo, 4, (mine - core + 2) // 2)
                reach = jnp.clip(reach - spans[0], 0, len(spans))
                for count in range(1, len(spans) + 1):

                    @pl.when(reach == count)
                    def _():
                        add(block_ref, rel, step, count)


def join(lengths_ref, own_ref, other_ref, out_ref):
    core = lax.axis_index("core")
    zlo = lax.axis_index("zlo")
    offset = lax.axis_index("zhi") * SLICE
    for step in range(4):
        live = lengths_ref[zlo * 8 + 2 * step + core]
        first_peak = own_ref[0, step, HD + 8 : HD + 9, :]
        second_peak = other_ref[step, HD + 8 : HD + 9, :]
        peak = jnp.maximum(first_peak, second_peak)
        first = jnp.exp2((first_peak - peak) * SCALE)
        second = jnp.exp2((second_peak - peak) * SCALE)
        total = own_ref[0, step, HD : HD + 1, :] * first + other_ref[step, HD : HD + 1, :] * second
        numerator = own_ref[0, step, :HD, :] * first + other_ref[step, :HD, :] * second
        result = (numerator / total).T
        row = lax.broadcasted_iota(jnp.int32, (SLICE, HD), 0)
        for piece in range(4):
            part = result[piece * SLICE : (piece + 1) * SLICE]
            part = jnp.where(row < live - piece * ROWS - offset, part, 0.0)
            out_ref[4 * step + piece] = part.astype(jnp.bfloat16)


def call(kernel, out_shape, in_specs, scratch=(), flops=0, moved=0, **kw):
    spec = pl.BlockSpec(memory_space=VMEM)
    return pl.pallas_call(
        kernel,
        out_shape=out_shape,
        in_specs=in_specs,
        out_specs=jax.tree.map(lambda _: spec, out_shape),
        scratch_shapes=list(scratch),
        compiler_params=pltpu.CompilerParams(vmem_limit_bytes=40 * 2**20),
        cost_estimate=pl.CostEstimate(flops=flops, bytes_accessed=moved, transcendentals=0),
        **kw,
    )


def shards(qkv, lengths):
    vmem = pl.BlockSpec(memory_space=VMEM)
    smem = pl.BlockSpec(memory_space=pltpu.SMEM)
    heads = 16
    bf16 = jnp.bfloat16
    with jax.named_scope("pack"):
        pairs, queries = call(
            pack,
            [
                jax.ShapeDtypeStruct((heads, 2 * SLICE, HD), bf16),
                jax.ShapeDtypeStruct((heads, SLICE, HD), bf16),
            ],
            [vmem],
        )(qkv[:, 0])
    with jax.named_scope("pairs_to_heads"):
        pairs = lax.all_to_all(pairs, ("y", "x"), 0, 0, tiled=True)
    with jax.named_scope("queries_to_heads"):
        queries = lax.all_to_all(queries, ("y", "x"), 0, 0, tiled=True)

    chips = 8
    place = [z % 2 * 4 + z // 2 for z in range(chips)]
    up = [(place[z], place[(z + 1) % chips]) for z in range(chips)]
    down = [(place[z], place[(z - 1) % chips]) for z in range(chips)]

    def swap(block):
        return lax.ppermute(block, "core", [(0, 1), (1, 0)])

    own = queries.reshape(4, ROWS, HD)
    with jax.named_scope("swap_queries"):
        other = swap(own)
    state_shape = jax.ShapeDtypeStruct((2, 4, STATE, ROWS), jnp.float32)

    def step(arrivals, sources, state):
        first = state is None
        operands = [lengths, own, other] + arrivals + ([] if first else [state])
        count = sum(a.shape[0] // 4 for a in arrivals)
        return call(
            functools.partial(attend, sources, first),
            state_shape,
            [smem] + [vmem] * (len(operands) - 1),
            [pltpu.VMEM((STATE, count * ROWS), bf16)],
            flops=4 * HD * ROWS * ROWS * 8 * count * 4,
            moved=8 * 2**20,
            input_output_aliases={} if first else {len(operands) - 1: 0},
        )(*operands)

    from_below, from_above = pairs, pairs
    state = None
    arrived = [pairs]
    sources = [(0, 0)]
    for distance in range(1, 6):
        if distance < 4:
            with jax.named_scope("ring"):
                from_below = lax.ppermute(from_below, RING, up)
                from_above = lax.ppermute(from_above, RING, down)
        elif distance == 4:
            half = heads // 2
            with jax.named_scope("ring"):
                from_below = lax.ppermute(from_below[:half], RING, up)
                from_above = lax.ppermute(from_above[half:], RING, down)
        with jax.named_scope("attend"):
            state = step(arrived, tuple(sources), state)
        arrived = [from_below, from_above]
        sources = [(-distance, 0), (distance, 0 if distance < 4 else 2)]
    with jax.named_scope("swap_terms"):
        theirs = swap(state[1])
    with jax.named_scope("join"):
        attended = call(
            join,
            jax.ShapeDtypeStruct((heads, SLICE, HD), bf16),
            [smem, vmem, vmem],
        )(lengths, state, theirs)
    with jax.named_scope("heads_to_tokens"):
        attended = lax.all_to_all(attended, ("y", "x"), 0, 0, tiled=True)
    with jax.named_scope("unpack"):
        out = call(unpack, jax.ShapeDtypeStruct((SLICE, heads * HD), bf16), [vmem])(attended)
    return out[None]


def solution(mesh):
    fine = Mesh(mesh.devices.reshape(2, 4, 2, 4, 4), ("zlo", "y", "core", "x", "zhi"))
    span, seq = ("zlo", "y", "core"), ("x", "zhi")
    return jax.shard_map(
        shards,
        mesh=fine,
        in_specs=(P(None, span, seq, None), P()),
        out_specs=P(span, seq, None),
        check_vma=False,
    )
```

```python
import functools
import math

import jax
import jax.numpy as jnp
from jax import lax
from jax.experimental import pallas as pl
from jax.experimental.pallas import tpu as pltpu
from jax.sharding import Mesh
from jax.sharding import PartitionSpec as P

HD = 128
SLICE = 64
ROWS = 256
FILL = -1e30
EXTRA = 16
STATE = HD + EXTRA
SCALE = math.log2(math.e) / math.sqrt(HD)
VMEM = pltpu.VMEM
RING = ("zlo", "zhi")


def pack(qkv_ref, pair_ref, query_ref):
    for head in range(query_ref.shape[0]):
        columns = slice(head * HD, (head + 1) * HD)
        query_ref[head] = qkv_ref[0, :, columns]
        pair_ref[head, :SLICE] = qkv_ref[1, :, columns]
        pair_ref[head, SLICE:] = qkv_ref[2, :, columns]


def unpack(parts_ref, out_ref):
    for head in range(parts_ref.shape[0]):
        out_ref[:, head * HD : (head + 1) * HD] = parts_ref[head]


def attend(sources, first, *refs):
    refs = list(refs)
    lengths_ref, own_ref, other_ref = refs[:3]
    arrivals = refs[3 : 3 + len(sources)]
    before_ref = None if first else refs[3 + len(sources)]
    state_ref, keys_ref, values_ref, turned_ref = refs[-4:]
    core = lax.axis_index("core")
    zlo = lax.axis_index("zlo")
    zed = lax.axis_index("zhi") * 2 + zlo
    pieces = []
    for number, (distance, begin) in enumerate(sources):
        for place in range(arrivals[number].shape[0] // 4):
            pieces.append((place + begin, number, place))
    pieces.sort()
    source_zed = [lax.rem(zed + 8 + distance, 8) for distance, _ in sources]
    source_zlo = lax.rem(source_zed[0], 2)
    groups = turned_ref.shape[1] // ROWS

    if first:
        state_ref[:, :, : HD + 8] = jnp.zeros_like(state_ref[:, :, : HD + 8])
        state_ref[:, :, HD + 8 :] = jnp.full_like(state_ref[:, :, HD + 8 :], FILL)
    else:
        state_ref[...] = before_ref[...]

    @pl.when(source_zlo <= zlo)
    def _():
        lane = lax.broadcasted_iota(jnp.int32, (SLICE, HD), 1)
        row = lax.broadcasted_iota(jnp.int32, (SLICE, HD), 0)
        count = jnp.int32(0)
        counts = {0: count}
        for span, number, place in pieces:
            live = lengths_ref[source_zlo * 8 + 2 * span + core]
            for part in range(4):
                bound = live - part * ROWS - (source_zed[number] // 2) * SLICE
                at = pl.ds(pl.multiple_of(count * SLICE, SLICE), SLICE)

                def lay():
                    block = arrivals[number].at[4 * place + part]
                    marks = (lane == span) | ((lane == 4) & (row >= bound))
                    keys_ref[at, :HD] = block[:SLICE, :]
                    keys_ref[at, HD:] = jnp.where(marks, 1.0, 0.0).astype(jnp.bfloat16)
                    values_ref[at, :] = block[SLICE:, :]

                if part < 2:
                    lay()
                    count = count + 1
                else:
                    pl.when(bound > 0)(lay)
                    count = count + jnp.where(bound > 0, 1, 0)
            counts[span + 1] = count
        rest = pl.ds(pl.multiple_of(count * SLICE, SLICE), 3 * SLICE)
        wide = lax.broadcasted_iota(jnp.int32, (3 * SLICE, HD), 1)
        keys_ref[rest, :HD] = jnp.zeros((3 * SLICE, HD), jnp.bfloat16)
        keys_ref[rest, HD:] = jnp.where(wide == 4, 1.0, 0.0).astype(jnp.bfloat16)
        values_ref[rest, :] = jnp.zeros((3 * SLICE, HD), jnp.bfloat16)
        ones = jnp.where(lax.broadcasted_iota(jnp.int32, (EXTRA, ROWS), 0) < 8, 1.0, 0.0)
        for group in range(groups):

            @pl.when(group * 4 < count)
            def _():
                columns = slice(group * ROWS, (group + 1) * ROWS)
                turned_ref[:HD, columns] = values_ref[columns, :].T
                turned_ref[HD:, columns] = ones.astype(jnp.bfloat16)

        def add(block_ref, rel, step, reach, used):
            lanes = lax.broadcasted_iota(jnp.int32, (ROWS, HD), 1)
            closed = jnp.where(lanes >= reach, FILL, 0.0).astype(jnp.bfloat16)
            queries = jnp.concatenate([block_ref[step], closed], axis=1)
            scores = lax.dot_general(
                keys_ref[: used * ROWS, :],
                queries,
                (((1,), (1,)), ((), ())),
                preferred_element_type=jnp.float32,
            )
            old_peak = state_ref[rel, step, HD + 8 : HD + 9, :]
            peak = jnp.maximum(old_peak, jnp.max(scores, axis=0, keepdims=True))
            weights = jnp.exp2((scores - peak) * SCALE).astype(jnp.bfloat16)
            fresh = jnp.dot(
                turned_ref[:, : used * ROWS], weights, preferred_element_type=jnp.float32
            )
            keep = jnp.exp2((old_peak - peak) * SCALE)
            state_ref[rel, step, : HD + 8, :] = (
                state_ref[rel, step, : HD + 8, :] * keep + fresh[: HD + 8]
            )
            state_ref[rel, step, HD + 8 :, :] = jnp.broadcast_to(peak, (8, ROWS))

        for rel, block_ref in ((0, own_ref), (1, other_ref)):

            @pl.loop(0, 4)
            def _(step):
                mine = 2 * step + (core if rel == 0 else 1 - core)
                reach = jnp.where(source_zlo < zlo, 4, (mine - core + 2) // 2)
                slices = jnp.int32(0)
                for span, total in counts.items():
                    slices = jnp.where(reach >= span, total, slices)
                used_groups = (slices + 3) // 4
                for used in range(1, groups + 1):

                    @pl.when(used_groups == used)
                    def _():
                        add(block_ref, rel, step, reach, used)


def join(lengths_ref, own_ref, other_ref, out_ref):
    core = lax.axis_index("core")
    zlo = lax.axis_index("zlo")
    offset = lax.axis_index("zhi") * SLICE
    for step in range(4):
        live = lengths_ref[zlo * 8 + 2 * step + core]
        first_peak = own_ref[0, step, HD + 8 : HD + 9, :]
        second_peak = other_ref[step, HD + 8 : HD + 9, :]
        peak = jnp.maximum(first_peak, second_peak)
        first = jnp.exp2((first_peak - peak) * SCALE)
        second = jnp.exp2((second_peak - peak) * SCALE)
        total = own_ref[0, step, HD : HD + 1, :] * first + other_ref[step, HD : HD + 1, :] * second
        numerator = own_ref[0, step, :HD, :] * first + other_ref[step, :HD, :] * second
        result = (numerator / total).T
        row = lax.broadcasted_iota(jnp.int32, (SLICE, HD), 0)
        for piece in range(4):
            part = result[piece * SLICE : (piece + 1) * SLICE]
            part = jnp.where(row < live - piece * ROWS - offset, part, 0.0)
            out_ref[4 * step + piece] = part.astype(jnp.bfloat16)


def call(kernel, out_shape, in_specs, scratch=(), flops=0, moved=0, **kw):
    spec = pl.BlockSpec(memory_space=VMEM)
    return pl.pallas_call(
        kernel,
        out_shape=out_shape,
        in_specs=in_specs,
        out_specs=jax.tree.map(lambda _: spec, out_shape),
        scratch_shapes=list(scratch),
        compiler_params=pltpu.CompilerParams(vmem_limit_bytes=40 * 2**20),
        cost_estimate=pl.CostEstimate(flops=flops, bytes_accessed=moved, transcendentals=0),
        **kw,
    )


def shards(qkv, lengths):
    vmem = pl.BlockSpec(memory_space=VMEM)
    smem = pl.BlockSpec(memory_space=pltpu.SMEM)
    heads = 16
    bf16 = jnp.bfloat16
    with jax.named_scope("pack"):
        pairs, queries = call(
            pack,
            [
                jax.ShapeDtypeStruct((heads, 2 * SLICE, HD), bf16),
                jax.ShapeDtypeStruct((heads, SLICE, HD), bf16),
            ],
            [vmem],
        )(qkv[:, 0])
    with jax.named_scope("pairs_to_heads"):
        pairs = lax.all_to_all(pairs, ("y", "x"), 0, 0, tiled=True)
    pairs, queries = lax.optimization_barrier((pairs, queries))
    with jax.named_scope("queries_to_heads"):
        queries = lax.all_to_all(queries, ("y", "x"), 0, 0, tiled=True)

    chips = 8
    place = [z % 2 * 4 + z // 2 for z in range(chips)]
    up = [(place[z], place[(z + 1) % chips]) for z in range(chips)]
    down = [(place[z], place[(z - 1) % chips]) for z in range(chips)]

    def swap(block):
        return lax.ppermute(block, "core", [(0, 1), (1, 0)])

    own = queries.reshape(4, ROWS, HD)
    with jax.named_scope("swap_queries"):
        other = swap(own)
    state_shape = jax.ShapeDtypeStruct((2, 4, STATE, ROWS), jnp.float32)

    def step(arrivals, sources, state):
        first = state is None
        operands = [lengths, own, other] + arrivals + ([] if first else [state])
        count = sum(a.shape[0] // 4 for a in arrivals)
        return call(
            functools.partial(attend, sources, first),
            state_shape,
            [smem] + [vmem] * (len(operands) - 1),
            [
                pltpu.VMEM((count * ROWS + 3 * SLICE, 2 * HD), bf16),
                pltpu.VMEM((count * ROWS + 3 * SLICE, HD), bf16),
                pltpu.VMEM((STATE, count * ROWS), bf16),
            ],
            flops=0 if first else 4 * HD * ROWS * ROWS * 8 * count * 4,
            moved=0 if first else 8 * 2**20,
            input_output_aliases={} if first else {len(operands) - 1: 0},
        )(*operands)

    from_below, from_above = pairs, pairs
    state = None
    arrived = [pairs]
    sources = [(0, 0)]
    for distance in range(1, 6):
        if distance < 4:
            with jax.named_scope("ring"):
                from_below = lax.ppermute(from_below, RING, up)
                from_above = lax.ppermute(from_above, RING, down)
        elif distance == 4:
            half = heads // 2
            with jax.named_scope("ring"):
                from_below = lax.ppermute(from_below[:half], RING, up)
                from_above = lax.ppermute(from_above[half:], RING, down)
        with jax.named_scope("attend"):
            state = step(arrived, tuple(sources), state)
        arrived = [from_below, from_above]
        sources = [(-distance, 0), (distance, 0 if distance < 4 else 2)]
    with jax.named_scope("swap_terms"):
        theirs = swap(state[1])
    with jax.named_scope("join"):
        attended = call(
            join,
            jax.ShapeDtypeStruct((heads, SLICE, HD), bf16),
            [smem, vmem, vmem],
        )(lengths, state, theirs)
    with jax.named_scope("heads_to_tokens"):
        attended = lax.all_to_all(attended, ("y", "x"), 0, 0, tiled=True)
    with jax.named_scope("unpack"):
        out = call(unpack, jax.ShapeDtypeStruct((SLICE, heads * HD), bf16), [vmem])(attended)
    return out[None]


def solution(mesh):
    fine = Mesh(mesh.devices.reshape(2, 4, 2, 4, 4), ("zlo", "y", "core", "x", "zhi"))
    span, seq = ("zlo", "y", "core"), ("x", "zhi")
    return jax.shard_map(
        shards,
        mesh=fine,
        in_specs=(P(None, span, seq, None), P()),
        out_specs=P(span, seq, None),
        check_vma=False,
    )
```

```python
import functools
import math

import jax
import jax.numpy as jnp
from jax import lax
from jax.experimental import pallas as pl
from jax.experimental.pallas import tpu as pltpu
from jax.sharding import Mesh
from jax.sharding import PartitionSpec as P

HD = 128
SLICE = 64
ROWS = 256
FILL = -1e30
STATE = HD + 16
SCALE = math.log2(math.e) / math.sqrt(HD)
VMEM = pltpu.VMEM
RING = ("zlo", "zhi")


def pack(qkv_ref, out_ref):
    for head in range(out_ref.shape[0]):
        columns = slice(head * HD, (head + 1) * HD)
        for part in range(3):
            out_ref[head, part * SLICE : (part + 1) * SLICE] = qkv_ref[part, :, columns]


def unpack(parts_ref, out_ref):
    for head in range(parts_ref.shape[0]):
        out_ref[:, head * HD : (head + 1) * HD] = parts_ref[head]


def split(parts_ref, query_ref, pair_ref):
    for span in range(4):
        block = parts_ref.at[4 * span : 4 * span + 4]
        query_ref[span] = block[:, :SLICE, :].reshape(ROWS, HD)
        pair_ref[span, :ROWS] = block[:, SLICE : 2 * SLICE, :].reshape(ROWS, HD)
        turned = block[:, 2 * SLICE :, :].reshape(ROWS, HD).T
        pair_ref[span, ROWS : ROWS + HD] = turned[:, :HD]
        pair_ref[span, ROWS + HD :] = turned[:, HD:]


def attend(sources, first, *refs):
    refs = list(refs)
    lengths_ref, own_ref, other_ref = refs[:3]
    arrivals = refs[3 : 3 + len(sources)]
    before_ref = None if first else refs[3 + len(sources)]
    state_ref = refs[-1]
    core = lax.axis_index("core")
    zlo = lax.axis_index("zlo")
    zed = lax.axis_index("zhi") * 2 + zlo
    pieces = []
    for number, (distance, begin) in enumerate(sources):
        for place in range(arrivals[number].shape[0]):
            pieces.append((place + begin, number, place))
    pieces.sort()
    source_zed = [lax.rem(zed + 8 + distance, 8) for distance, _ in sources]
    source_zlo = lax.rem(source_zed[0], 2)
    aligned = sources[0][0] % 2 == 0

    if first:
        state_ref[:, : HD + 8] = jnp.zeros_like(state_ref[:, : HD + 8])
        state_ref[:, HD + 8 :] = jnp.full_like(state_ref[:, HD + 8 :], FILL)
    else:
        state_ref[...] = before_ref[...]

    ones = jnp.where(lax.broadcasted_iota(jnp.int32, (16, ROWS), 0) < 8, 1.0, 0.0)
    ones = ones.astype(jnp.bfloat16)

    def add(step, count, last):
        queries = jnp.concatenate([own_ref[step], other_ref[step]], axis=0)
        scores, values = [], []
        for span, number, place in pieces:
            if span >= count:
                continue
            block = arrivals[number].at[place]
            score = lax.dot_general(
                block[:ROWS, :], queries, (((1,), (1,)), ((), ())), preferred_element_type=jnp.float32
            )
            live = lengths_ref[source_zlo * 8 + 2 * span + core]
            offset = (source_zed[number] // 2) * SLICE
            row = lax.broadcasted_iota(jnp.int32, (SLICE, 2 * ROWS), 0)
            other_half = lax.broadcasted_iota(jnp.int32, (SLICE, 2 * ROWS), 1) >= ROWS
            for part in range(4):
                rows = score[part * SLICE : (part + 1) * SLICE]
                bound = live - part * ROWS - offset
                if span == last:
                    bound = jnp.where(other_half, jnp.where(core == 1, 0, bound), bound)
                    rows = jnp.where(row < bound, rows, FILL)
                elif part >= 2:
                    rows = jnp.where(row < bound, rows, FILL)
                scores.append(rows)
            turned = jnp.concatenate([block[ROWS : ROWS + HD, :], block[ROWS + HD :, :]], axis=1)
            values.append(jnp.concatenate([turned, ones], axis=0))
        scores = jnp.concatenate(scores, axis=0)
        old_peak = state_ref[step, HD + 8 : HD + 9, :]
        peak = jnp.maximum(old_peak, jnp.max(scores, axis=0, keepdims=True))
        shifted = (scores - peak) * SCALE
        weights = jnp.exp2(shifted)
        if last == 0:
            weights = jnp.where(scores > FILL, weights, 0.0)
        weights = weights.astype(jnp.bfloat16)
        fresh = jnp.dot(
            jnp.concatenate(values, axis=1), weights, preferred_element_type=jnp.float32
        )
        keep = jnp.exp2((old_peak - peak) * SCALE)
        state_ref[step, : HD + 8, :] = state_ref[step, : HD + 8, :] * keep + fresh[: HD + 8]
        state_ref[step, HD + 8 :, :] = jnp.broadcast_to(peak, (8, 2 * ROWS))

    if aligned:
        for step in range(4):
            add(step, step + 1, step)
    else:

        @pl.when(source_zlo < zlo)
        def _():
            @pl.loop(0, 4)
            def _(step):
                add(step, 4, -1)


def join(lengths_ref, own_ref, other_ref, out_ref):
    core = lax.axis_index("core")
    zlo = lax.axis_index("zlo")
    offset = lax.axis_index("zhi") * SLICE
    for step in range(4):
        live = lengths_ref[zlo * 8 + 2 * step + core]
        first_peak = own_ref[step, HD + 8 : HD + 9, :ROWS]
        second_peak = other_ref[step, HD + 8 : HD + 9, :]
        peak = jnp.maximum(first_peak, second_peak)
        first = jnp.exp2((first_peak - peak) * SCALE)
        second = jnp.exp2((second_peak - peak) * SCALE)
        total = own_ref[step, HD : HD + 1, :ROWS] * first + other_ref[step, HD : HD + 1, :] * second
        numerator = own_ref[step, :HD, :ROWS] * first + other_ref[step, :HD, :] * second
        result = (numerator / total).T
        row = lax.broadcasted_iota(jnp.int32, (SLICE, HD), 0)
        for piece in range(4):
            part = result[piece * SLICE : (piece + 1) * SLICE]
            part = jnp.where(row < live - piece * ROWS - offset, part, 0.0)
            out_ref[4 * step + piece] = part.astype(jnp.bfloat16)


def call(kernel, out_shape, in_specs, flops=0, moved=0, **kw):
    spec = pl.BlockSpec(memory_space=VMEM)
    return pl.pallas_call(
        kernel,
        out_shape=out_shape,
        in_specs=in_specs,
        out_specs=jax.tree.map(lambda _: spec, out_shape),
        compiler_params=pltpu.CompilerParams(vmem_limit_bytes=40 * 2**20),
        cost_estimate=pl.CostEstimate(flops=flops, bytes_accessed=moved, transcendentals=0),
        **kw,
    )


def shards(qkv, lengths):
    vmem = pl.BlockSpec(memory_space=VMEM)
    smem = pl.BlockSpec(memory_space=pltpu.SMEM)
    heads = 16
    bf16 = jnp.bfloat16
    with jax.named_scope("pack"):
        parts = call(pack, jax.ShapeDtypeStruct((heads, 3 * SLICE, HD), bf16), [vmem])(qkv[:, 0])
    with jax.named_scope("tokens_to_heads"):
        parts = lax.all_to_all(parts, ("y", "x"), 0, 0, tiled=True)
    with jax.named_scope("split"):
        own, pairs = call(
            split,
            [
                jax.ShapeDtypeStruct((4, ROWS, HD), bf16),
                jax.ShapeDtypeStruct((4, 2 * ROWS, HD), bf16),
            ],
            [vmem],
        )(parts)

    chips = 8
    place = [z % 2 * 4 + z // 2 for z in range(chips)]
    up = [(place[z], place[(z + 1) % chips]) for z in range(chips)]
    down = [(place[z], place[(z - 1) % chips]) for z in range(chips)]

    def swap(block):
        return lax.ppermute(block, "core", [(0, 1), (1, 0)])

    with jax.named_scope("swap_queries"):
        other = swap(own)
    state_shape = jax.ShapeDtypeStruct((4, STATE, 2 * ROWS), jnp.float32)

    def step(arrivals, sources, state):
        first = state is None
        operands = [lengths, own, other] + arrivals + ([] if first else [state])
        count = sum(a.shape[0] for a in arrivals)
        return call(
            functools.partial(attend, sources, first),
            state_shape,
            [smem] + [vmem] * (len(operands) - 1),
            flops=4 * HD * ROWS * ROWS * 8 * count * 4,
            moved=8 * 2**20,
            input_output_aliases={} if first else {len(operands) - 1: 0},
        )(*operands)

    from_below, from_above = pairs, pairs
    state = None
    arrived = [pairs]
    sources = [(0, 0)]
    for distance in range(1, 6):
        with jax.named_scope("ring"):
            if distance < 4:
                from_below = lax.ppermute(from_below, RING, up)
                from_above = lax.ppermute(from_above, RING, down)
            elif distance == 4:
                from_below = lax.ppermute(from_below[:2], RING, up)
                from_above = lax.ppermute(from_above[2:], RING, down)
        with jax.named_scope("attend"):
            state = step(arrived, tuple(sources), state)
        arrived = [from_below, from_above]
        sources = [(-distance, 0), (distance, 0 if distance < 4 else 2)]
    with jax.named_scope("swap_terms"):
        theirs = swap(state[:, :, ROWS:])
    with jax.named_scope("join"):
        attended = call(
            join,
            jax.ShapeDtypeStruct((heads, SLICE, HD), bf16),
            [smem, vmem, vmem],
        )(lengths, state, theirs)
    with jax.named_scope("heads_to_tokens"):
        attended = lax.all_to_all(attended, ("y", "x"), 0, 0, tiled=True)
    with jax.named_scope("unpack"):
        out = call(unpack, jax.ShapeDtypeStruct((SLICE, heads * HD), bf16), [vmem])(attended)
    return out[None]


def solution(mesh):
    fine = Mesh(mesh.devices.reshape(2, 4, 2, 4, 4), ("zlo", "y", "core", "x", "zhi"))
    span, seq = ("zlo", "y", "core"), ("x", "zhi")
    return jax.shard_map(
        shards,
        mesh=fine,
        in_specs=(P(None, span, seq, None), P()),
        out_specs=P(span, seq, None),
        check_vma=False,
    )
```

```python
import functools
import math

import jax
import jax.numpy as jnp
from jax import lax
from jax.experimental import pallas as pl
from jax.experimental.pallas import tpu as pltpu
from jax.sharding import Mesh
from jax.sharding import PartitionSpec as P

HD = 128
SLICE = 64
ROWS = 256
FILL = -1e30
STATE = HD + 16
SCALE = math.log2(math.e) / math.sqrt(HD)
VMEM = pltpu.VMEM
RING = ("zlo", "zhi")


def pack(qkv_ref, out_ref):
    for head in range(out_ref.shape[0]):
        columns = slice(head * HD, (head + 1) * HD)
        for part in range(3):
            out_ref[head, part * SLICE : (part + 1) * SLICE] = qkv_ref[part, :, columns]


def unpack(parts_ref, out_ref):
    for head in range(parts_ref.shape[0]):
        out_ref[:, head * HD : (head + 1) * HD] = parts_ref[head]


def split(parts_ref, query_ref, key_ref, value_ref):
    for span in range(4):
        block = parts_ref.at[4 * span : 4 * span + 4]
        query_ref[span] = block[:, :SLICE, :].reshape(ROWS, HD)
        key_ref[span] = block[:, SLICE : 2 * SLICE, :].reshape(ROWS, HD)
        turned = block[:, 2 * SLICE :, :].reshape(ROWS, HD).T
        value_ref[span, :HD] = turned[:, :HD]
        value_ref[span, HD:] = turned[:, HD:]


def attend(sources, first, *refs):
    refs = list(refs)
    lengths_ref, own_ref, other_ref = refs[:3]
    key_refs = refs[3 : 3 + len(sources)]
    value_refs = refs[3 + len(sources) : 3 + 2 * len(sources)]
    before_ref = None if first else refs[-2]
    state_ref = refs[-1]
    core = lax.axis_index("core")
    zlo = lax.axis_index("zlo")
    zed = lax.axis_index("zhi") * 2 + zlo
    pieces = []
    for number, (distance, begin) in enumerate(sources):
        for place in range(key_refs[number].shape[0]):
            pieces.append((place + begin, number, place))
    pieces.sort()
    source_zed = [lax.rem(zed + 8 + distance, 8) for distance, _ in sources]
    source_zlo = lax.rem(source_zed[0], 2)
    aligned = sources[0][0] % 2 == 0

    ones = jnp.where(lax.broadcasted_iota(jnp.int32, (16, ROWS), 0) < 8, 1.0, 0.0)
    ones = ones.astype(jnp.bfloat16)

    def add(step, count, last):
        queries = jnp.concatenate([own_ref[step], other_ref[step]], axis=0)
        scores, values = [], []
        for span, number, place in pieces:
            if span >= count:
                continue
            score = lax.dot_general(
                key_refs[number][place],
                queries,
                (((1,), (1,)), ((), ())),
                preferred_element_type=jnp.float32,
            )
            live = lengths_ref[source_zlo * 8 + 2 * span + core]
            offset = (source_zed[number] // 2) * SLICE
            row = lax.broadcasted_iota(jnp.int32, (SLICE, 2 * ROWS), 0)
            other_half = lax.broadcasted_iota(jnp.int32, (SLICE, 2 * ROWS), 1) >= ROWS
            for part in range(4):
                rows = score[part * SLICE : (part + 1) * SLICE]
                bound = live - part * ROWS - offset
                if span == last:
                    bound = jnp.where(other_half, jnp.where(core == 1, 0, bound), bound)
                    rows = jnp.where(row < bound, rows, FILL)
                elif part >= 2:
                    rows = jnp.where(row < bound, rows, FILL)
                scores.append(rows)
            block = value_refs[number].at[place]
            turned = jnp.concatenate([block[:HD, :], block[HD:, :]], axis=1)
            values.append(jnp.concatenate([turned, ones], axis=0))
        scores = jnp.concatenate(scores, axis=0)
        peak = jnp.max(scores, axis=0, keepdims=True)
        if not first:
            old_peak = before_ref[step, HD + 8 : HD + 9, :]
            peak = jnp.maximum(old_peak, peak)
        shifted = (scores - peak) * SCALE
        weights = jnp.exp2(shifted)
        if last == 0:
            weights = jnp.where(scores > FILL, weights, 0.0)
        weights = weights.astype(jnp.bfloat16)
        fresh = jnp.dot(
            jnp.concatenate(values, axis=1), weights, preferred_element_type=jnp.float32
        )
        fresh = fresh[: HD + 8]
        if not first:
            keep = jnp.exp2((old_peak - peak) * SCALE)
            fresh = before_ref[step, : HD + 8, :] * keep + fresh
        state_ref[step, : HD + 8, :] = fresh
        state_ref[step, HD + 8 :, :] = jnp.broadcast_to(peak, (8, 2 * ROWS))

    if aligned:
        for step in range(4):
            add(step, step + 1, step)
    else:

        @pl.when(source_zlo < zlo)
        def _():
            @pl.loop(0, 4)
            def _(step):
                add(step, 4, -1)

        @pl.when(source_zlo > zlo)
        def _():
            state_ref[...] = before_ref[...]


def join(lengths_ref, own_ref, other_ref, out_ref):
    core = lax.axis_index("core")
    zlo = lax.axis_index("zlo")
    offset = lax.axis_index("zhi") * SLICE
    for step in range(4):
        live = lengths_ref[zlo * 8 + 2 * step + core]
        first_peak = own_ref[step, HD + 8 : HD + 9, :ROWS]
        second_peak = other_ref[step, HD + 8 : HD + 9, :]
        peak = jnp.maximum(first_peak, second_peak)
        first = jnp.exp2((first_peak - peak) * SCALE)
        second = jnp.exp2((second_peak - peak) * SCALE)
        total = own_ref[step, HD : HD + 1, :ROWS] * first + other_ref[step, HD : HD + 1, :] * second
        numerator = own_ref[step, :HD, :ROWS] * first + other_ref[step, :HD, :] * second
        result = (numerator / total).T
        row = lax.broadcasted_iota(jnp.int32, (SLICE, HD), 0)
        for piece in range(4):
            part = result[piece * SLICE : (piece + 1) * SLICE]
            part = jnp.where(row < live - piece * ROWS - offset, part, 0.0)
            out_ref[4 * step + piece] = part.astype(jnp.bfloat16)


def call(kernel, out_shape, in_specs, flops=0, moved=0, **kw):
    spec = pl.BlockSpec(memory_space=VMEM)
    return pl.pallas_call(
        kernel,
        out_shape=out_shape,
        in_specs=in_specs,
        out_specs=jax.tree.map(lambda _: spec, out_shape),
        compiler_params=pltpu.CompilerParams(vmem_limit_bytes=40 * 2**20),
        cost_estimate=pl.CostEstimate(flops=flops, bytes_accessed=moved, transcendentals=0),
        **kw,
    )


def shards(qkv, lengths):
    vmem = pl.BlockSpec(memory_space=VMEM)
    smem = pl.BlockSpec(memory_space=pltpu.SMEM)
    heads = 16
    bf16 = jnp.bfloat16
    with jax.named_scope("pack"):
        parts = call(pack, jax.ShapeDtypeStruct((heads, 3 * SLICE, HD), bf16), [vmem])(qkv[:, 0])
    with jax.named_scope("tokens_to_heads"):
        parts = lax.all_to_all(parts, ("y", "x"), 0, 0, tiled=True)
    with jax.named_scope("split"):
        own, keys, values = call(split, [jax.ShapeDtypeStruct((4, ROWS, HD), bf16)] * 3, [vmem])(parts)

    chips = 8
    place = [z % 2 * 4 + z // 2 for z in range(chips)]
    up = [(place[z], place[(z + 1) % chips]) for z in range(chips)]
    down = [(place[z], place[(z - 1) % chips]) for z in range(chips)]

    def swap(block):
        return lax.ppermute(block, "core", [(0, 1), (1, 0)])

    with jax.named_scope("swap_queries"):
        other = swap(own)
    state_shape = jax.ShapeDtypeStruct((4, STATE, 2 * ROWS), jnp.float32)

    def step(keys, values, sources, state):
        first = state is None
        operands = [lengths, own, other] + keys + values + ([] if first else [state])
        count = sum(a.shape[0] for a in keys)
        return call(
            functools.partial(attend, sources, first),
            state_shape,
            [smem] + [vmem] * (len(operands) - 1),
            flops=4 * HD * ROWS * ROWS * 8 * count * 4,
            moved=8 * 2**20,
            input_output_aliases={} if first else {len(operands) - 1: 0},
        )(*operands)

    def hop(pair, distance):
        below, above = pair
        if distance == 4:
            below, above = below[:2], above[2:]
        return [lax.ppermute(below, RING, up), lax.ppermute(above, RING, down)]

    state = None
    held = ([keys], [values])
    moving = ([keys, keys], [values, values])
    sources = [(0, 0)]
    for distance in range(1, 6):
        if distance < 5:
            with jax.named_scope("ring"):
                moving = tuple(hop(pair, distance) for pair in moving)
        with jax.named_scope("attend"):
            state = step(*held, tuple(sources), state)
        held = moving
        sources = [(-distance, 0), (distance, 0 if distance < 4 else 2)]
    with jax.named_scope("swap_terms"):
        theirs = swap(state[:, :, ROWS:])
    with jax.named_scope("join"):
        attended = call(
            join,
            jax.ShapeDtypeStruct((heads, SLICE, HD), bf16),
            [smem, vmem, vmem],
        )(lengths, state, theirs)
    with jax.named_scope("heads_to_tokens"):
        attended = lax.all_to_all(attended, ("y", "x"), 0, 0, tiled=True)
    with jax.named_scope("unpack"):
        out = call(unpack, jax.ShapeDtypeStruct((SLICE, heads * HD), bf16), [vmem])(attended)
    return out[None]


def solution(mesh):
    fine = Mesh(mesh.devices.reshape(2, 4, 2, 4, 4), ("zlo", "y", "core", "x", "zhi"))
    span, seq = ("zlo", "y", "core"), ("x", "zhi")
    return jax.shard_map(
        shards,
        mesh=fine,
        in_specs=(P(None, span, seq, None), P()),
        out_specs=P(span, seq, None),
        check_vma=False,
    )
```

```python
import functools
import math

import jax
import jax.numpy as jnp
from jax import lax
from jax.experimental import pallas as pl
from jax.experimental.pallas import tpu as pltpu
from jax.sharding import Mesh
from jax.sharding import PartitionSpec as P

HD = 128
SLICE = 64
ROWS = 256
FILL = -1e30
STATE = HD + 16
SCALE = math.log2(math.e) / math.sqrt(HD)
VMEM = pltpu.VMEM
RING = ("zlo", "zhi")


def pack(qkv_ref, out_ref):
    for head in range(out_ref.shape[0]):
        columns = slice(head * HD, (head + 1) * HD)
        for part in range(3):
            out_ref[head, part * SLICE : (part + 1) * SLICE] = qkv_ref[part, :, columns]


def unpack(parts_ref, out_ref):
    for head in range(parts_ref.shape[0]):
        out_ref[:, head * HD : (head + 1) * HD] = parts_ref[head]


def split(parts_ref, query_ref, *pair_refs):
    for span in range(4):
        block = parts_ref.at[4 * span : 4 * span + 4]
        pair_ref = pair_refs[span // 2].at[span % 2]
        query_ref[span] = block[:, :SLICE, :].reshape(ROWS, HD)
        pair_ref[:ROWS] = block[:, SLICE : 2 * SLICE, :].reshape(ROWS, HD)
        turned = block[:, 2 * SLICE :, :].reshape(ROWS, HD).T
        pair_ref[ROWS : ROWS + HD] = turned[:, :HD]
        pair_ref[ROWS + HD :] = turned[:, HD:]


def attend(sources, first, *refs):
    refs = list(refs)
    lengths_ref, own_ref, other_ref = refs[:3]
    arrivals = refs[3 : 3 + len(sources)]
    before_ref = None if first else refs[-2]
    state_ref = refs[-1]
    core = lax.axis_index("core")
    zlo = lax.axis_index("zlo")
    zed = lax.axis_index("zhi") * 2 + zlo
    pieces = []
    for number, (distance, begin) in enumerate(sources):
        for place in range(arrivals[number].shape[0]):
            pieces.append((place + begin, number, place))
    pieces.sort()
    source_zed = [lax.rem(zed + 8 + distance, 8) for distance, _ in sources]
    source_zlo = lax.rem(source_zed[0], 2)
    aligned = sources[0][0] % 2 == 0

    ones = jnp.where(lax.broadcasted_iota(jnp.int32, (16, ROWS), 0) < 8, 1.0, 0.0)
    ones = ones.astype(jnp.bfloat16)

    def add(step, count, last):
        queries = jnp.concatenate([own_ref[step], other_ref[step]], axis=0)
        scores, values = [], []
        for span, number, place in pieces:
            if span >= count:
                continue
            block = arrivals[number].at[place]
            score = lax.dot_general(
                block[:ROWS, :],
                queries,
                (((1,), (1,)), ((), ())),
                preferred_element_type=jnp.float32,
            )
            live = lengths_ref[source_zlo * 8 + 2 * span + core]
            offset = (source_zed[number] // 2) * SLICE
            row = lax.broadcasted_iota(jnp.int32, (SLICE, 2 * ROWS), 0)
            other_half = lax.broadcasted_iota(jnp.int32, (SLICE, 2 * ROWS), 1) >= ROWS
            for part in range(4):
                rows = score[part * SLICE : (part + 1) * SLICE]
                bound = live - part * ROWS - offset
                if span == last:
                    bound = jnp.where(other_half, jnp.where(core == 1, 0, bound), bound)
                    rows = jnp.where(row < bound, rows, FILL)
                elif part >= 2:
                    rows = jnp.where(row < bound, rows, FILL)
                scores.append(rows)
            turned = jnp.concatenate([block[ROWS : ROWS + HD, :], block[ROWS + HD :, :]], axis=1)
            values.append(jnp.concatenate([turned, ones], axis=0))
        scores = jnp.concatenate(scores, axis=0)
        peak = jnp.max(scores, axis=0, keepdims=True)
        if not first:
            old_peak = before_ref[step, HD + 8 : HD + 9, :]
            peak = jnp.maximum(old_peak, peak)
        shifted = (scores - peak) * SCALE
        weights = jnp.exp2(shifted)
        if last == 0:
            weights = jnp.where(scores > FILL, weights, 0.0)
        weights = weights.astype(jnp.bfloat16)
        fresh = jnp.dot(
            jnp.concatenate(values, axis=1), weights, preferred_element_type=jnp.float32
        )
        fresh = fresh[: HD + 8]
        if not first:
            keep = jnp.exp2((old_peak - peak) * SCALE)
            fresh = before_ref[step, : HD + 8, :] * keep + fresh
        state_ref[step, : HD + 8, :] = fresh
        state_ref[step, HD + 8 :, :] = jnp.broadcast_to(peak, (8, 2 * ROWS))

    if aligned:
        for step in range(4):
            add(step, step + 1, step)
    else:

        @pl.when(source_zlo < zlo)
        def _():
            @pl.loop(0, 4, unroll=2)
            def _(step):
                add(step, 4, -1)

        @pl.when(source_zlo > zlo)
        def _():
            state_ref[...] = before_ref[...]


def join(lengths_ref, own_ref, other_ref, out_ref):
    core = lax.axis_index("core")
    zlo = lax.axis_index("zlo")
    offset = lax.axis_index("zhi") * SLICE
    for step in range(4):
        live = lengths_ref[zlo * 8 + 2 * step + core]
        first_peak = own_ref[step, HD + 8 : HD + 9, :ROWS]
        second_peak = other_ref[step, HD + 8 : HD + 9, :]
        peak = jnp.maximum(first_peak, second_peak)
        first = jnp.exp2((first_peak - peak) * SCALE)
        second = jnp.exp2((second_peak - peak) * SCALE)
        total = own_ref[step, HD : HD + 1, :ROWS] * first + other_ref[step, HD : HD + 1, :] * second
        numerator = own_ref[step, :HD, :ROWS] * first + other_ref[step, :HD, :] * second
        result = (numerator / total).T
        row = lax.broadcasted_iota(jnp.int32, (SLICE, HD), 0)
        for piece in range(4):
            part = result[piece * SLICE : (piece + 1) * SLICE]
            part = jnp.where(row < live - piece * ROWS - offset, part, 0.0)
            out_ref[4 * step + piece] = part.astype(jnp.bfloat16)


def call(kernel, out_shape, in_specs, flops=0, moved=0, **kw):
    spec = pl.BlockSpec(memory_space=VMEM)
    return pl.pallas_call(
        kernel,
        out_shape=out_shape,
        in_specs=in_specs,
        out_specs=jax.tree.map(lambda _: spec, out_shape),
        compiler_params=pltpu.CompilerParams(vmem_limit_bytes=40 * 2**20),
        cost_estimate=pl.CostEstimate(flops=flops, bytes_accessed=moved, transcendentals=0),
        **kw,
    )


def shards(qkv, lengths):
    vmem = pl.BlockSpec(memory_space=VMEM)
    smem = pl.BlockSpec(memory_space=pltpu.SMEM)
    heads = 16
    bf16 = jnp.bfloat16
    with jax.named_scope("pack"):
        parts = call(pack, jax.ShapeDtypeStruct((heads, 3 * SLICE, HD), bf16), [vmem])(qkv[:, 0])
    with jax.named_scope("tokens_to_heads"):
        parts = lax.all_to_all(parts, ("y", "x"), 0, 0, tiled=True)
    with jax.named_scope("split"):
        own, *pairs = call(
            split,
            [jax.ShapeDtypeStruct((4, ROWS, HD), bf16)]
            + [jax.ShapeDtypeStruct((2, 2 * ROWS, HD), bf16)] * 2,
            [vmem],
        )(parts)

    chips = 8
    place = [z % 2 * 4 + z // 2 for z in range(chips)]
    up = [(place[z], place[(z + 1) % chips]) for z in range(chips)]
    down = [(place[z], place[(z - 1) % chips]) for z in range(chips)]

    def swap(block):
        return lax.ppermute(block, "core", [(0, 1), (1, 0)])

    with jax.named_scope("swap_queries"):
        other = swap(own)
    state_shape = jax.ShapeDtypeStruct((4, STATE, 2 * ROWS), jnp.float32)

    def step(arrivals, sources, state):
        first = state is None
        operands = [lengths, own, other] + arrivals + ([] if first else [state])
        count = sum(a.shape[0] for a in arrivals)
        return call(
            functools.partial(attend, sources, first),
            state_shape,
            [smem] + [vmem] * (len(operands) - 1),
            flops=4 * HD * ROWS * ROWS * 8 * count * 4,
            moved=8 * 2**20,
            input_output_aliases={} if first else {len(operands) - 1: 0},
        )(*operands)

    def hop(below, above):
        with jax.named_scope("ring"):
            return (
                [lax.ppermute(block, RING, up) for block in below],
                [lax.ppermute(block, RING, down) for block in above],
            )

    below, above = hop(pairs, pairs)
    with jax.named_scope("attend"):
        state = step(pairs, ((0, 0), (0, 2)), None)
    below[0], state = lax.optimization_barrier((below[0], state))
    for distance in range(1, 5):
        arrived = below + above
        if distance < 4:
            sources = ((-distance, 0), (-distance, 2), (distance, 0), (distance, 2))
        else:
            sources = ((-distance, 0), (distance, 2))
        if distance < 3:
            below, above = hop(below, above)
        elif distance == 3:
            below, above = hop(below[:1], above[1:])
        with jax.named_scope("attend"):
            state = step(arrived, sources, state)
    with jax.named_scope("swap_terms"):
        theirs = swap(state[:, :, ROWS:])
    with jax.named_scope("join"):
        attended = call(
            join,
            jax.ShapeDtypeStruct((heads, SLICE, HD), bf16),
            [smem, vmem, vmem],
        )(lengths, state, theirs)
    with jax.named_scope("heads_to_tokens"):
        attended = lax.all_to_all(attended, ("y", "x"), 0, 0, tiled=True)
    with jax.named_scope("unpack"):
        out = call(unpack, jax.ShapeDtypeStruct((SLICE, heads * HD), bf16), [vmem])(attended)
    return out[None]


def solution(mesh):
    fine = Mesh(mesh.devices.reshape(2, 4, 2, 4, 4), ("zlo", "y", "core", "x", "zhi"))
    span, seq = ("zlo", "y", "core"), ("x", "zhi")
    return jax.shard_map(
        shards,
        mesh=fine,
        in_specs=(P(None, span, seq, None), P()),
        out_specs=P(span, seq, None),
        check_vma=False,
    )
```

```python
import functools
import math

import jax
import jax.numpy as jnp
from jax import lax
from jax.experimental import pallas as pl
from jax.experimental.pallas import tpu as pltpu
from jax.sharding import Mesh
from jax.sharding import PartitionSpec as P

HD = 128
SLICE = 64
ROWS = 256
FILL = -1e30
STATE = HD + 16
SCALE = math.log2(math.e) / math.sqrt(HD)
VMEM = pltpu.VMEM
RING = ("zlo", "core", "zhi")


def pack(qkv_ref, out_ref):
    for head in range(out_ref.shape[0]):
        columns = slice(head * HD, (head + 1) * HD)
        for part in range(3):
            out_ref[head, part * SLICE : (part + 1) * SLICE] = qkv_ref[part, :, columns]


def unpack(parts_ref, out_ref):
    for head in range(parts_ref.shape[0]):
        out_ref[:, head * HD : (head + 1) * HD] = parts_ref[head]


def split(parts_ref, query_ref, pair_ref):
    for span in range(4):
        block = parts_ref.at[4 * span : 4 * span + 4]
        query_ref[span] = block[:, :SLICE, :].reshape(ROWS, HD)
        pair_ref[span, :ROWS] = block[:, SLICE : 2 * SLICE, :].reshape(ROWS, HD)
        turned = block[:, 2 * SLICE :, :].reshape(ROWS, HD).T
        pair_ref[span, ROWS : ROWS + HD] = turned[:, :HD]
        pair_ref[span, ROWS + HD :] = turned[:, HD:]


def attend(distance, first, *refs):
    refs = list(refs)
    lengths_ref, own_ref, other_ref = refs[:3]
    arrivals = refs[3:-1] if first else refs[3:-2]
    before_ref = None if first else refs[-2]
    state_ref = refs[-1]
    core = lax.axis_index("core")
    zlo = lax.axis_index("zlo")
    zed = lax.axis_index("zhi") * 2 + zlo
    pieces = [(span, number) for span in range(4) for number in range(len(arrivals))]
    source_zed = lax.rem(zed + 8 + jnp.where(core == 0, -distance, distance), 8)
    source_zlo = lax.rem(source_zed, 2)
    source_core = [core, 1 - core]
    offset = (source_zed // 2) * SLICE
    aligned = distance % 2 == 0

    ones = jnp.where(lax.broadcasted_iota(jnp.int32, (16, ROWS), 0) < 8, 1.0, 0.0)
    ones = ones.astype(jnp.bfloat16)

    def add(step, count, last):
        queries = jnp.concatenate([own_ref[step], other_ref[step]], axis=0)
        scores, values = [], []
        for span, number in pieces:
            if span >= count:
                continue
            block = arrivals[number].at[span]
            score = lax.dot_general(
                block[:ROWS, :],
                queries,
                (((1,), (1,)), ((), ())),
                preferred_element_type=jnp.float32,
            )
            live = lengths_ref[source_zlo * 8 + 2 * span + source_core[number]]
            row = lax.broadcasted_iota(jnp.int32, (SLICE, 2 * ROWS), 0)
            other_half = lax.broadcasted_iota(jnp.int32, (SLICE, 2 * ROWS), 1) >= ROWS
            for part in range(4):
                rows = score[part * SLICE : (part + 1) * SLICE]
                bound = live - part * ROWS - offset
                if span == last:
                    own_bound = jnp.where(source_core[number] <= core, bound, 0)
                    other_bound = jnp.where(source_core[number] <= 1 - core, bound, 0)
                    bound = jnp.where(other_half, other_bound, own_bound)
                    rows = jnp.where(row < bound, rows, FILL)
                elif part >= 2:
                    rows = jnp.where(row < bound, rows, FILL)
                scores.append(rows)
            turned = jnp.concatenate([block[ROWS : ROWS + HD, :], block[ROWS + HD :, :]], axis=1)
            values.append(jnp.concatenate([turned, ones], axis=0))
        scores = jnp.concatenate(scores, axis=0)
        peak = jnp.max(scores, axis=0, keepdims=True)
        if not first:
            old_peak = before_ref[step, HD + 8 : HD + 9, :]
            peak = jnp.maximum(old_peak, peak)
        shifted = (scores - peak) * SCALE
        weights = jnp.exp2(shifted)
        if last == 0:
            weights = jnp.where(scores > FILL, weights, 0.0)
        weights = weights.astype(jnp.bfloat16)
        fresh = jnp.dot(
            jnp.concatenate(values, axis=1), weights, preferred_element_type=jnp.float32
        )
        fresh = fresh[: HD + 8]
        if not first:
            keep = jnp.exp2((old_peak - peak) * SCALE)
            fresh = before_ref[step, : HD + 8, :] * keep + fresh
        state_ref[step, : HD + 8, :] = fresh
        state_ref[step, HD + 8 :, :] = jnp.broadcast_to(peak, (8, 2 * ROWS))

    if aligned:
        for step in range(4):
            add(step, step + 1, step)
    else:

        @pl.when(source_zlo < zlo)
        def _():
            @pl.loop(0, 4, unroll=2)
            def _(step):
                add(step, 4, -1)

        @pl.when(source_zlo > zlo)
        def _():
            state_ref[...] = before_ref[...]


def join(lengths_ref, own_ref, other_ref, out_ref):
    core = lax.axis_index("core")
    zlo = lax.axis_index("zlo")
    offset = lax.axis_index("zhi") * SLICE
    for step in range(4):
        live = lengths_ref[zlo * 8 + 2 * step + core]
        first_peak = own_ref[step, HD + 8 : HD + 9, :ROWS]
        second_peak = other_ref[step, HD + 8 : HD + 9, :]
        peak = jnp.maximum(first_peak, second_peak)
        first = jnp.exp2((first_peak - peak) * SCALE)
        second = jnp.exp2((second_peak - peak) * SCALE)
        total = own_ref[step, HD : HD + 1, :ROWS] * first + other_ref[step, HD : HD + 1, :] * second
        numerator = own_ref[step, :HD, :ROWS] * first + other_ref[step, :HD, :] * second
        result = (numerator / total).T
        row = lax.broadcasted_iota(jnp.int32, (SLICE, HD), 0)
        for piece in range(4):
            part = result[piece * SLICE : (piece + 1) * SLICE]
            part = jnp.where(row < live - piece * ROWS - offset, part, 0.0)
            out_ref[4 * step + piece] = part.astype(jnp.bfloat16)


def call(kernel, out_shape, in_specs, flops=0, moved=0, **kw):
    spec = pl.BlockSpec(memory_space=VMEM)
    return pl.pallas_call(
        kernel,
        out_shape=out_shape,
        in_specs=in_specs,
        out_specs=jax.tree.map(lambda _: spec, out_shape),
        compiler_params=pltpu.CompilerParams(vmem_limit_bytes=40 * 2**20),
        cost_estimate=pl.CostEstimate(flops=flops, bytes_accessed=moved, transcendentals=0),
        **kw,
    )


def shards(qkv, lengths):
    vmem = pl.BlockSpec(memory_space=VMEM)
    smem = pl.BlockSpec(memory_space=pltpu.SMEM)
    heads = 16
    bf16 = jnp.bfloat16
    with jax.named_scope("pack"):
        parts = call(pack, jax.ShapeDtypeStruct((heads, 3 * SLICE, HD), bf16), [vmem])(qkv[:, 0])
    with jax.named_scope("tokens_to_heads"):
        parts = lax.all_to_all(parts, ("y", "x"), 0, 0, tiled=True)
    with jax.named_scope("split"):
        own, pairs = call(
            split,
            [
                jax.ShapeDtypeStruct((4, ROWS, HD), bf16),
                jax.ShapeDtypeStruct((4, 2 * ROWS, HD), bf16),
            ],
            [vmem],
        )(parts)

    chips = 8
    place = [z % 2 * 8 + z // 2 for z in range(chips)]
    route = [(place[z], place[(z + 1) % chips]) for z in range(chips)]
    route += [(place[z] + 4, place[(z - 1) % chips] + 4) for z in range(chips)]

    def hop(block):
        with jax.named_scope("ring"):
            return lax.ppermute(block, RING, route)

    def swap(block):
        return lax.ppermute(block, "core", [(0, 1), (1, 0)])

    first_chain = hop(pairs)
    with jax.named_scope("swap_queries"):
        other = swap(own)
    with jax.named_scope("swap_pairs"):
        second = swap(pairs)
    other, second = lax.optimization_barrier((other, second))
    second_chain = hop(second)
    state_shape = jax.ShapeDtypeStruct((4, STATE, 2 * ROWS), jnp.float32)

    def step(arrivals, distance, state):
        first = state is None
        operands = [lengths, own, other] + arrivals + ([] if first else [state])
        count = 4 * len(arrivals)
        with jax.named_scope("attend"):
            return call(
                functools.partial(attend, distance, first),
                state_shape,
                [smem] + [vmem] * (len(operands) - 1),
                flops=4 * HD * ROWS * ROWS * 8 * count * 4,
                moved=8 * 2**20,
                input_output_aliases={} if first else {len(operands) - 1: 0},
            )(*operands)

    state = step([pairs], 0, None)
    for distance in range(1, 4):
        first_chain, state = lax.optimization_barrier((first_chain, state))
        second_chain, state = lax.optimization_barrier((second_chain, state))
        arrived = [first_chain, second_chain]
        first_chain = hop(first_chain)
        if distance < 3:
            second_chain = hop(second_chain)
        state = step(arrived, distance, state)
    state = step([first_chain], 4, state)
    with jax.named_scope("swap_terms"):
        theirs = swap(state[:, :, ROWS:])
    with jax.named_scope("join"):
        attended = call(
            join,
            jax.ShapeDtypeStruct((heads, SLICE, HD), bf16),
            [smem, vmem, vmem],
        )(lengths, state, theirs)
    with jax.named_scope("heads_to_tokens"):
        attended = lax.all_to_all(attended, ("y", "x"), 0, 0, tiled=True)
    with jax.named_scope("unpack"):
        out = call(unpack, jax.ShapeDtypeStruct((SLICE, heads * HD), bf16), [vmem])(attended)
    return out[None]


def solution(mesh):
    fine = Mesh(mesh.devices.reshape(2, 4, 2, 4, 4), ("zlo", "y", "core", "x", "zhi"))
    span, seq = ("zlo", "y", "core"), ("x", "zhi")
    return jax.shard_map(
        shards,
        mesh=fine,
        in_specs=(P(None, span, seq, None), P()),
        out_specs=P(span, seq, None),
        check_vma=False,
    )
```

```python
import functools
import math

import jax
import jax.numpy as jnp
from jax import lax
from jax.experimental import pallas as pl
from jax.experimental.pallas import tpu as pltpu
from jax.sharding import Mesh
from jax.sharding import PartitionSpec as P

HD = 128
SLICE = 64
ROWS = 256
FILL = -1e30
STATE = HD + 16
SCALE = math.log2(math.e) / math.sqrt(HD)
VMEM = pltpu.VMEM
RING = ("zlo", "core", "zhi")


def pack(qkv_ref, out_ref):
    for head in range(out_ref.shape[0]):
        columns = slice(head * HD, (head + 1) * HD)
        for part in range(3):
            out_ref[head, part * SLICE : (part + 1) * SLICE] = qkv_ref[part, :, columns]


def unpack(parts_ref, out_ref):
    for head in range(parts_ref.shape[0]):
        out_ref[:, head * HD : (head + 1) * HD] = parts_ref[head]


def split(parts_ref, query_ref, pair_ref):
    for span in range(4):
        block = parts_ref.at[4 * span : 4 * span + 4]
        query_ref[span] = block[:, :SLICE, :].reshape(ROWS, HD)
        pair_ref[span, :ROWS] = block[:, SLICE : 2 * SLICE, :].reshape(ROWS, HD)
        turned = block[:, 2 * SLICE :, :].reshape(ROWS, HD).T
        pair_ref[span, ROWS : ROWS + HD] = turned[:, :HD]
        pair_ref[span, ROWS + HD :] = turned[:, HD:]


def attend(distance, parts, first, *refs):
    refs = list(refs)
    lengths_ref, own_ref, other_ref = refs[:3]
    arrivals = refs[3:-1] if first else refs[3:-2]
    before_ref = None if first else refs[-2]
    state_ref = refs[-1]
    core = lax.axis_index("core")
    zlo = lax.axis_index("zlo")
    zed = lax.axis_index("zhi") * 2 + zlo
    pieces = []
    for number, (_, begin) in enumerate(parts):
        for place in range(arrivals[number].shape[0]):
            pieces.append((place + begin, number, place))
    pieces.sort()
    source_zed = lax.rem(zed + 8 + jnp.where(core == 0, -distance, distance), 8)
    source_zlo = lax.rem(source_zed, 2)
    source_core = [core if chain == 0 else 1 - core for chain, _ in parts]
    offset = (source_zed // 2) * SLICE
    aligned = distance % 2 == 0

    ones = jnp.where(lax.broadcasted_iota(jnp.int32, (16, ROWS), 0) < 8, 1.0, 0.0)
    ones = ones.astype(jnp.bfloat16)

    def add(step, count, last):
        queries = jnp.concatenate([own_ref[step], other_ref[step]], axis=0)
        scores, values = [], []
        for span, number, place in pieces:
            if span >= count:
                continue
            block = arrivals[number].at[place]
            score = lax.dot_general(
                block[:ROWS, :],
                queries,
                (((1,), (1,)), ((), ())),
                preferred_element_type=jnp.float32,
            )
            live = lengths_ref[source_zlo * 8 + 2 * span + source_core[number]]
            row = lax.broadcasted_iota(jnp.int32, (SLICE, 2 * ROWS), 0)
            other_half = lax.broadcasted_iota(jnp.int32, (SLICE, 2 * ROWS), 1) >= ROWS
            for part in range(4):
                rows = score[part * SLICE : (part + 1) * SLICE]
                bound = live - part * ROWS - offset
                if span == last:
                    own_bound = jnp.where(source_core[number] <= core, bound, 0)
                    other_bound = jnp.where(source_core[number] <= 1 - core, bound, 0)
                    bound = jnp.where(other_half, other_bound, own_bound)
                    rows = jnp.where(row < bound, rows, FILL)
                elif part >= 2:
                    rows = jnp.where(row < bound, rows, FILL)
                scores.append(rows)
            turned = jnp.concatenate([block[ROWS : ROWS + HD, :], block[ROWS + HD :, :]], axis=1)
            values.append(jnp.concatenate([turned, ones], axis=0))
        if not scores:
            state_ref[step] = before_ref[step]
            return
        scores = jnp.concatenate(scores, axis=0)
        peak = jnp.max(scores, axis=0, keepdims=True)
        if not first:
            old_peak = before_ref[step, HD + 8 : HD + 9, :]
            peak = jnp.maximum(old_peak, peak)
        shifted = (scores - peak) * SCALE
        weights = jnp.exp2(shifted)
        if last == 0:
            weights = jnp.where(scores > FILL, weights, 0.0)
        weights = weights.astype(jnp.bfloat16)
        fresh = jnp.dot(
            jnp.concatenate(values, axis=1), weights, preferred_element_type=jnp.float32
        )
        fresh = fresh[: HD + 8]
        if not first:
            keep = jnp.exp2((old_peak - peak) * SCALE)
            fresh = before_ref[step, : HD + 8, :] * keep + fresh
        state_ref[step, : HD + 8, :] = fresh
        state_ref[step, HD + 8 :, :] = jnp.broadcast_to(peak, (8, 2 * ROWS))

    if aligned:
        for step in range(4):
            add(step, step + 1, step)
    else:

        @pl.when(source_zlo < zlo)
        def _():
            @pl.loop(0, 4, unroll=2)
            def _(step):
                add(step, 4, -1)

        @pl.when(source_zlo > zlo)
        def _():
            state_ref[...] = before_ref[...]


def join(lengths_ref, own_ref, other_ref, out_ref):
    core = lax.axis_index("core")
    zlo = lax.axis_index("zlo")
    offset = lax.axis_index("zhi") * SLICE
    for step in range(4):
        live = lengths_ref[zlo * 8 + 2 * step + core]
        first_peak = own_ref[step, HD + 8 : HD + 9, :ROWS]
        second_peak = other_ref[step, HD + 8 : HD + 9, :]
        peak = jnp.maximum(first_peak, second_peak)
        first = jnp.exp2((first_peak - peak) * SCALE)
        second = jnp.exp2((second_peak - peak) * SCALE)
        total = own_ref[step, HD : HD + 1, :ROWS] * first + other_ref[step, HD : HD + 1, :] * second
        numerator = own_ref[step, :HD, :ROWS] * first + other_ref[step, :HD, :] * second
        result = (numerator / total).T
        row = lax.broadcasted_iota(jnp.int32, (SLICE, HD), 0)
        for piece in range(4):
            part = result[piece * SLICE : (piece + 1) * SLICE]
            part = jnp.where(row < live - piece * ROWS - offset, part, 0.0)
            out_ref[4 * step + piece] = part.astype(jnp.bfloat16)


def call(kernel, out_shape, in_specs, flops=0, moved=0, **kw):
    spec = pl.BlockSpec(memory_space=VMEM)
    return pl.pallas_call(
        kernel,
        out_shape=out_shape,
        in_specs=in_specs,
        out_specs=jax.tree.map(lambda _: spec, out_shape),
        compiler_params=pltpu.CompilerParams(vmem_limit_bytes=40 * 2**20),
        cost_estimate=pl.CostEstimate(flops=flops, bytes_accessed=moved, transcendentals=0),
        **kw,
    )


def shards(qkv, lengths):
    vmem = pl.BlockSpec(memory_space=VMEM)
    smem = pl.BlockSpec(memory_space=pltpu.SMEM)
    heads = 16
    bf16 = jnp.bfloat16
    with jax.named_scope("pack"):
        parts = call(pack, jax.ShapeDtypeStruct((heads, 3 * SLICE, HD), bf16), [vmem])(qkv[:, 0])
    with jax.named_scope("tokens_to_heads"):
        parts = lax.all_to_all(parts, ("y", "x"), 0, 0, tiled=True)
    with jax.named_scope("split"):
        own, pairs = call(
            split,
            [
                jax.ShapeDtypeStruct((4, ROWS, HD), bf16),
                jax.ShapeDtypeStruct((4, 2 * ROWS, HD), bf16),
            ],
            [vmem],
        )(parts)

    chips = 8
    place = [z % 2 * 8 + z // 2 for z in range(chips)]
    route = [(place[z], place[(z + 1) % chips]) for z in range(chips)]
    route += [(place[z] + 4, place[(z - 1) % chips] + 4) for z in range(chips)]

    def hop(block):
        with jax.named_scope("ring"):
            return lax.ppermute(block, RING, route)

    def swap(block):
        return lax.ppermute(block, "core", [(0, 1), (1, 0)])

    with jax.named_scope("swap_queries"):
        other = swap(own)
    with jax.named_scope("swap_pairs"):
        second = swap(pairs)
    first_chain = hop(pairs)
    other, second = lax.optimization_barrier((other, second))
    second_chain = hop(second)
    state_shape = jax.ShapeDtypeStruct((4, STATE, 2 * ROWS), jnp.float32)

    def step(arrivals, distance, parts, state):
        first = state is None
        operands = [lengths, own, other] + arrivals + ([] if first else [state])
        count = sum(a.shape[0] for a in arrivals)
        with jax.named_scope("attend"):
            return call(
                functools.partial(attend, distance, parts, first),
                state_shape,
                [smem] + [vmem] * (len(operands) - 1),
                flops=4 * HD * ROWS * ROWS * 8 * count * 4,
                moved=8 * 2**20,
                input_output_aliases={} if first else {len(operands) - 1: 0},
            )(*operands)

    def after(block, state):
        return lax.optimization_barrier((block, state))

    state = step([pairs], 0, ((0, 0),), None)
    for distance in range(1, 3):
        first_chain, state = after(first_chain, state)
        second_chain, state = after(second_chain, state)
        arrived = [first_chain, second_chain]
        first_chain, second_chain = hop(first_chain), hop(second_chain)
        state = step(arrived, distance, ((0, 0), (1, 0)), state)
    first_chain, state = after(first_chain, state)
    halves = [hop(first_chain[:2]), hop(first_chain[2:])]
    state = step([first_chain], 3, ((0, 0),), state)
    second_chain, state = after(second_chain, state)
    state = step([second_chain], 3, ((1, 0),), state)
    for number in range(2):
        block, state = after(halves[number], state)
        state = step([block], 4, ((0, 2 * number),), state)
    with jax.named_scope("swap_terms"):
        theirs = swap(state[:, :, ROWS:])
    with jax.named_scope("join"):
        attended = call(
            join,
            jax.ShapeDtypeStruct((heads, SLICE, HD), bf16),
            [smem, vmem, vmem],
        )(lengths, state, theirs)
    with jax.named_scope("heads_to_tokens"):
        attended = lax.all_to_all(attended, ("y", "x"), 0, 0, tiled=True)
    with jax.named_scope("unpack"):
        out = call(unpack, jax.ShapeDtypeStruct((SLICE, heads * HD), bf16), [vmem])(attended)
    return out[None]


def solution(mesh):
    fine = Mesh(mesh.devices.reshape(2, 4, 2, 4, 4), ("zlo", "y", "core", "x", "zhi"))
    span, seq = ("zlo", "y", "core"), ("x", "zhi")
    return jax.shard_map(
        shards,
        mesh=fine,
        in_specs=(P(None, span, seq, None), P()),
        out_specs=P(span, seq, None),
        check_vma=False,
    )
```

```python
import functools
import math

import jax
import jax.numpy as jnp
from jax import lax
from jax.experimental import pallas as pl
from jax.experimental.pallas import tpu as pltpu
from jax.sharding import Mesh
from jax.sharding import PartitionSpec as P

HD = 128
SLICE = 64
ROWS = 256
FILL = -1e30
STATE = HD + 16
SCALE = math.log2(math.e) / math.sqrt(HD)
VMEM = pltpu.VMEM
RING = ("zlo", "core", "zhi")


def pack(qkv_ref, out_ref):
    for head in range(out_ref.shape[0]):
        columns = slice(head * HD, (head + 1) * HD)
        for part in range(3):
            out_ref[head, part * SLICE : (part + 1) * SLICE] = qkv_ref[part, :, columns]


def unpack(parts_ref, out_ref):
    for head in range(parts_ref.shape[0]):
        out_ref[:, head * HD : (head + 1) * HD] = parts_ref[head]


def split(parts_ref, query_ref, pair_ref):
    for span in range(4):
        block = parts_ref.at[4 * span : 4 * span + 4]
        query_ref[span] = block[:, :SLICE, :].reshape(ROWS, HD)
        pair_ref[span, :ROWS] = block[:, SLICE : 2 * SLICE, :].reshape(ROWS, HD)
        turned = block[:, 2 * SLICE :, :].reshape(ROWS, HD).T
        pair_ref[span, ROWS : ROWS + HD] = turned[:, :HD]
        pair_ref[span, ROWS + HD :] = turned[:, HD:]


def attend(distance, first, half, *refs):
    refs = list(refs)
    lengths_ref, own_ref, other_ref = refs[:3]
    arrivals = refs[3:-1] if first else refs[3:-2]
    before_ref = None if first else refs[-2]
    state_ref = refs[-1]
    core = lax.axis_index("core")
    zlo = lax.axis_index("zlo")
    zed = lax.axis_index("zhi") * 2 + zlo
    pieces = [(span, number) for span in range(4) for number in range(len(arrivals))]
    source_zed = lax.rem(zed + 8 + jnp.where(core == 0, -distance, distance), 8)
    source_zlo = lax.rem(source_zed, 2)
    source_core = [core, 1 - core]
    offset = (source_zed // 2) * SLICE
    aligned = distance % 2 == 0

    width = state_ref.shape[2]
    columns = slice(ROWS if half == 1 else 0, ROWS if half == 0 else 2 * ROWS)

    ones = jnp.where(lax.broadcasted_iota(jnp.int32, (16, ROWS), 0) < 8, 1.0, 0.0)
    ones = ones.astype(jnp.bfloat16)

    def add(step, count, last):
        if half is None:
            queries = jnp.concatenate([own_ref[step], other_ref[step]], axis=0)
        else:
            queries = (own_ref, other_ref)[half][step]
        scores, values = [], []
        for span, number in pieces:
            if span >= count:
                continue
            block = arrivals[number].at[span]
            score = lax.dot_general(
                block[:ROWS, :],
                queries,
                (((1,), (1,)), ((), ())),
                preferred_element_type=jnp.float32,
            )
            live = lengths_ref[source_zlo * 8 + 2 * span + source_core[number]]
            row = lax.broadcasted_iota(jnp.int32, (SLICE, width), 0)
            other_half = lax.broadcasted_iota(jnp.int32, (SLICE, width), 1) >= ROWS
            for part in range(4):
                rows = score[part * SLICE : (part + 1) * SLICE]
                bound = live - part * ROWS - offset
                if span == last:
                    own_bound = jnp.where(source_core[number] <= core, bound, 0)
                    other_bound = jnp.where(source_core[number] <= 1 - core, bound, 0)
                    if half is None:
                        bound = jnp.where(other_half, other_bound, own_bound)
                    else:
                        bound = (own_bound, other_bound)[half]
                    rows = jnp.where(row < bound, rows, FILL)
                elif part >= 2:
                    rows = jnp.where(row < bound, rows, FILL)
                scores.append(rows)
            turned = jnp.concatenate([block[ROWS : ROWS + HD, :], block[ROWS + HD :, :]], axis=1)
            values.append(jnp.concatenate([turned, ones], axis=0))
        scores = jnp.concatenate(scores, axis=0)
        peak = jnp.max(scores, axis=0, keepdims=True)
        if not first:
            old_peak = before_ref[step, HD + 8 : HD + 9, columns]
            peak = jnp.maximum(old_peak, peak)
        shifted = (scores - peak) * SCALE
        weights = jnp.exp2(shifted)
        if last == 0:
            weights = jnp.where(scores > FILL, weights, 0.0)
        weights = weights.astype(jnp.bfloat16)
        fresh = jnp.dot(
            jnp.concatenate(values, axis=1), weights, preferred_element_type=jnp.float32
        )
        fresh = fresh[: HD + 8]
        if not first:
            keep = jnp.exp2((old_peak - peak) * SCALE)
            fresh = before_ref[step, : HD + 8, columns] * keep + fresh
        state_ref[step, : HD + 8, :] = fresh
        state_ref[step, HD + 8 :, :] = jnp.broadcast_to(peak, (8, width))

    if aligned:
        for step in range(4):
            add(step, step + 1, step)
    else:

        @pl.when(source_zlo < zlo)
        def _():
            @pl.loop(0, 4, unroll=2)
            def _(step):
                add(step, 4, -1)

        @pl.when(source_zlo > zlo)
        def _():
            state_ref[...] = before_ref[...]


def join(lengths_ref, own_ref, other_ref, out_ref):
    core = lax.axis_index("core")
    zlo = lax.axis_index("zlo")
    offset = lax.axis_index("zhi") * SLICE
    for step in range(4):
        live = lengths_ref[zlo * 8 + 2 * step + core]
        first_peak = own_ref[step, HD + 8 : HD + 9, :]
        second_peak = other_ref[step, HD + 8 : HD + 9, :]
        peak = jnp.maximum(first_peak, second_peak)
        first = jnp.exp2((first_peak - peak) * SCALE)
        second = jnp.exp2((second_peak - peak) * SCALE)
        total = own_ref[step, HD : HD + 1, :] * first + other_ref[step, HD : HD + 1, :] * second
        numerator = own_ref[step, :HD, :] * first + other_ref[step, :HD, :] * second
        result = (numerator / total).T
        row = lax.broadcasted_iota(jnp.int32, (SLICE, HD), 0)
        for piece in range(4):
            part = result[piece * SLICE : (piece + 1) * SLICE]
            part = jnp.where(row < live - piece * ROWS - offset, part, 0.0)
            out_ref[4 * step + piece] = part.astype(jnp.bfloat16)


def call(kernel, out_shape, in_specs, flops=0, moved=0, **kw):
    spec = pl.BlockSpec(memory_space=VMEM)
    return pl.pallas_call(
        kernel,
        out_shape=out_shape,
        in_specs=in_specs,
        out_specs=jax.tree.map(lambda _: spec, out_shape),
        compiler_params=pltpu.CompilerParams(vmem_limit_bytes=40 * 2**20),
        cost_estimate=pl.CostEstimate(flops=flops, bytes_accessed=moved, transcendentals=0),
        **kw,
    )


def shards(qkv, lengths):
    vmem = pl.BlockSpec(memory_space=VMEM)
    smem = pl.BlockSpec(memory_space=pltpu.SMEM)
    heads = 16
    bf16 = jnp.bfloat16
    with jax.named_scope("pack"):
        parts = call(pack, jax.ShapeDtypeStruct((heads, 3 * SLICE, HD), bf16), [vmem])(qkv[:, 0])
    with jax.named_scope("tokens_to_heads"):
        parts = lax.all_to_all(parts, ("y", "x"), 0, 0, tiled=True)
    with jax.named_scope("split"):
        own, pairs = call(
            split,
            [
                jax.ShapeDtypeStruct((4, ROWS, HD), bf16),
                jax.ShapeDtypeStruct((4, 2 * ROWS, HD), bf16),
            ],
            [vmem],
        )(parts)

    chips = 8
    place = [z % 2 * 8 + z // 2 for z in range(chips)]
    route = [(place[z], place[(z + 1) % chips]) for z in range(chips)]
    route += [(place[z] + 4, place[(z - 1) % chips] + 4) for z in range(chips)]

    across = [(place[z] + 4, place[(z + 1) % chips]) for z in range(chips)]
    across += [(place[z], place[(z - 1) % chips] + 4) for z in range(chips)]

    def hop(block, pairs=route):
        with jax.named_scope("ring"):
            return lax.ppermute(block, RING, pairs)

    def swap(block):
        return lax.ppermute(block, "core", [(0, 1), (1, 0)])

    first_chain = hop(pairs)
    with jax.named_scope("swap_queries"):
        other = swap(own)
    other, again = lax.optimization_barrier((other, pairs))
    second_chain = hop(again, across)

    def step(arrivals, distance, state, half=None):
        first = state is None
        operands = [lengths, own, other] + arrivals + ([] if first else [state])
        count = 4 * len(arrivals)
        width = 2 * ROWS if half is None else ROWS
        with jax.named_scope("attend"):
            return call(
                functools.partial(attend, distance, first, half),
                jax.ShapeDtypeStruct((4, STATE, width), jnp.float32),
                [smem] + [vmem] * (len(operands) - 1),
                flops=16 * HD * ROWS * width * 4 * count,
                moved=8 * 2**20,
                input_output_aliases={} if first or half is not None else {len(operands) - 1: 0},
            )(*operands)

    state = step([pairs], 0, None)
    for distance in range(1, 4):
        first_chain, state = lax.optimization_barrier((first_chain, state))
        second_chain, state = lax.optimization_barrier((second_chain, state))
        arrived = [first_chain, second_chain]
        first_chain = hop(first_chain)
        if distance < 3:
            second_chain = hop(second_chain)
        state = step(arrived, distance, state)
    theirs = step([first_chain], 4, state, 1)
    with jax.named_scope("swap_terms"):
        theirs = swap(theirs)
    mine = step([first_chain], 4, state, 0)
    with jax.named_scope("join"):
        attended = call(
            join,
            jax.ShapeDtypeStruct((heads, SLICE, HD), bf16),
            [smem, vmem, vmem],
        )(lengths, mine, theirs)
    with jax.named_scope("heads_to_tokens"):
        attended = lax.all_to_all(attended, ("y", "x"), 0, 0, tiled=True)
    with jax.named_scope("unpack"):
        out = call(unpack, jax.ShapeDtypeStruct((SLICE, heads * HD), bf16), [vmem])(attended)
    return out[None]


def solution(mesh):
    fine = Mesh(mesh.devices.reshape(2, 4, 2, 4, 4), ("zlo", "y", "core", "x", "zhi"))
    span, seq = ("zlo", "y", "core"), ("x", "zhi")
    return jax.shard_map(
        shards,
        mesh=fine,
        in_specs=(P(None, span, seq, None), P()),
        out_specs=P(span, seq, None),
        check_vma=False,
    )
```

```python
import functools
import math

import jax
import jax.numpy as jnp
from jax import lax
from jax.experimental import pallas as pl
from jax.experimental.pallas import tpu as pltpu
from jax.sharding import Mesh
from jax.sharding import PartitionSpec as P

HD = 128
SLICE = 64
ROWS = 256
FILL = -1e30
STATE = HD + 16
SCALE = math.log2(math.e) / math.sqrt(HD)
VMEM = pltpu.VMEM
RING = ("zlo", "core", "zhi")


def pack(qkv_ref, out_ref):
    for head in range(out_ref.shape[0]):
        columns = slice(head * HD, (head + 1) * HD)
        for part in range(3):
            out_ref[head, part * SLICE : (part + 1) * SLICE] = qkv_ref[part, :, columns]


def unpack(parts_ref, out_ref):
    for head in range(parts_ref.shape[0]):
        out_ref[:, head * HD : (head + 1) * HD] = parts_ref[head]


def split(parts_ref, query_ref, pair_ref):
    for span in range(4):
        block = parts_ref.at[4 * span : 4 * span + 4]
        query_ref[span] = block[:, :SLICE, :].reshape(ROWS, HD)
        pair_ref[span, :ROWS] = block[:, SLICE : 2 * SLICE, :].reshape(ROWS, HD)
        turned = block[:, 2 * SLICE :, :].reshape(ROWS, HD).T
        pair_ref[span, ROWS : ROWS + HD] = turned[:, :HD]
        pair_ref[span, ROWS + HD :] = turned[:, HD:]


def attend(distance, first, half, *refs):
    refs = list(refs)
    lengths_ref, own_ref, other_ref = refs[:3]
    arrivals = refs[3:-1] if first else refs[3:-2]
    before_ref = None if first else refs[-2]
    state_ref = refs[-1]
    core = lax.axis_index("core")
    zlo = lax.axis_index("zlo")
    zed = lax.axis_index("zhi") * 2 + zlo
    pieces = [(span, number) for span in range(4) for number in range(len(arrivals))]
    source_zed = lax.rem(zed + 8 + jnp.where(core == 0, -distance, distance), 8)
    source_zlo = lax.rem(source_zed, 2)
    source_core = [core, 1 - core]
    offset = (source_zed // 2) * SLICE
    aligned = distance % 2 == 0

    width = state_ref.shape[2]
    columns = slice(ROWS if half == 1 else 0, ROWS if half == 0 else 2 * ROWS)

    ones = jnp.where(lax.broadcasted_iota(jnp.int32, (16, ROWS), 0) < 8, 1.0, 0.0)
    ones = ones.astype(jnp.bfloat16)

    def add(step, count, last):
        if half is None:
            queries = jnp.concatenate([own_ref[step], other_ref[step]], axis=0)
        else:
            queries = (own_ref, other_ref)[half][step]
        scores, values = [], []
        for span, number in pieces:
            if span >= count:
                continue
            block = arrivals[number].at[span]
            score = lax.dot_general(
                block[:ROWS, :],
                queries,
                (((1,), (1,)), ((), ())),
                preferred_element_type=jnp.float32,
            )
            live = lengths_ref[source_zlo * 8 + 2 * span + source_core[number]]
            row = lax.broadcasted_iota(jnp.int32, (SLICE, width), 0)
            other_half = lax.broadcasted_iota(jnp.int32, (SLICE, width), 1) >= ROWS
            for part in range(4):
                rows = score[part * SLICE : (part + 1) * SLICE]
                bound = live - part * ROWS - offset
                if span == last:
                    own_bound = jnp.where(source_core[number] <= core, bound, 0)
                    other_bound = jnp.where(source_core[number] <= 1 - core, bound, 0)
                    if half is None:
                        bound = jnp.where(other_half, other_bound, own_bound)
                    else:
                        bound = (own_bound, other_bound)[half]
                    rows = jnp.where(row < bound, rows, FILL)
                elif part >= 2:
                    rows = jnp.where(row < bound, rows, FILL)
                scores.append(rows)
            turned = jnp.concatenate([block[ROWS : ROWS + HD, :], block[ROWS + HD :, :]], axis=1)
            values.append(jnp.concatenate([turned, ones], axis=0))
        scores = jnp.concatenate(scores, axis=0)
        peak = jnp.max(scores, axis=0, keepdims=True)
        if not first:
            old_peak = before_ref[step, HD + 8 : HD + 9, columns]
            peak = jnp.maximum(old_peak, peak)
        shifted = (scores - peak) * SCALE
        weights = jnp.exp2(shifted)
        if last == 0:
            weights = jnp.where(scores > FILL, weights, 0.0)
        weights = weights.astype(jnp.bfloat16)
        fresh = jnp.dot(
            jnp.concatenate(values, axis=1), weights, preferred_element_type=jnp.float32
        )
        fresh = fresh[: HD + 8]
        if not first:
            keep = jnp.exp2((old_peak - peak) * SCALE)
            fresh = before_ref[step, : HD + 8, columns] * keep + fresh
        state_ref[step, : HD + 8, :] = fresh
        state_ref[step, HD + 8 :, :] = jnp.broadcast_to(peak, (8, width))

    if aligned:
        for step in range(4):
            add(step, step + 1, step)
    else:

        @pl.when(source_zlo < zlo)
        def _():
            @pl.loop(0, 4, unroll=2)
            def _(step):
                add(step, 4, -1)

        @pl.when(source_zlo > zlo)
        def _():
            state_ref[...] = before_ref[...]


def join(lengths_ref, own_ref, other_ref, out_ref):
    core = lax.axis_index("core")
    zlo = lax.axis_index("zlo")
    offset = lax.axis_index("zhi") * SLICE
    for step in range(4):
        live = lengths_ref[zlo * 8 + 2 * step + core]
        first_peak = own_ref[step, HD + 8 : HD + 9, :]
        second_peak = other_ref[step, HD + 8 : HD + 9, :]
        peak = jnp.maximum(first_peak, second_peak)
        first = jnp.exp2((first_peak - peak) * SCALE)
        second = jnp.exp2((second_peak - peak) * SCALE)
        total = own_ref[step, HD : HD + 1, :] * first + other_ref[step, HD : HD + 1, :] * second
        numerator = own_ref[step, :HD, :] * first + other_ref[step, :HD, :] * second
        result = (numerator / total).T
        row = lax.broadcasted_iota(jnp.int32, (SLICE, HD), 0)
        for piece in range(4):
            part = result[piece * SLICE : (piece + 1) * SLICE]
            part = jnp.where(row < live - piece * ROWS - offset, part, 0.0)
            out_ref[4 * step + piece] = part.astype(jnp.bfloat16)


def call(kernel, out_shape, in_specs, flops=0, moved=0, **kw):
    spec = pl.BlockSpec(memory_space=VMEM)
    return pl.pallas_call(
        kernel,
        out_shape=out_shape,
        in_specs=in_specs,
        out_specs=jax.tree.map(lambda _: spec, out_shape),
        compiler_params=pltpu.CompilerParams(vmem_limit_bytes=40 * 2**20),
        cost_estimate=pl.CostEstimate(flops=flops, bytes_accessed=moved, transcendentals=0),
        **kw,
    )


def shards(qkv, lengths):
    vmem = pl.BlockSpec(memory_space=VMEM)
    smem = pl.BlockSpec(memory_space=pltpu.SMEM)
    heads = 16
    bf16 = jnp.bfloat16
    with jax.named_scope("pack"):
        parts = call(pack, jax.ShapeDtypeStruct((heads, 3 * SLICE, HD), bf16), [vmem])(qkv[:, 0])
    with jax.named_scope("tokens_to_heads"):
        parts = lax.all_to_all(parts, ("y", "x"), 0, 0, tiled=True)
    with jax.named_scope("split"):
        own, pairs = call(
            split,
            [
                jax.ShapeDtypeStruct((4, ROWS, HD), bf16),
                jax.ShapeDtypeStruct((4, 2 * ROWS, HD), bf16),
            ],
            [vmem],
        )(parts)

    chips = 8
    place = [z % 2 * 8 + z // 2 for z in range(chips)]
    route = [(place[z], place[(z + 1) % chips]) for z in range(chips)]
    route += [(place[z] + 4, place[(z - 1) % chips] + 4) for z in range(chips)]

    def hop(block):
        with jax.named_scope("ring"):
            return lax.ppermute(block, RING, route)

    def swap(block):
        return lax.ppermute(block, "core", [(0, 1), (1, 0)])

    first_chain = hop(pairs)
    with jax.named_scope("swap_queries"):
        other = swap(own)
    with jax.named_scope("swap_pairs"):
        second = swap(pairs)
    other, second = lax.optimization_barrier((other, second))
    second_chain = hop(second)

    def step(arrivals, distance, state, half=None):
        first = state is None
        operands = [lengths, own, other] + arrivals + ([] if first else [state])
        count = 4 * len(arrivals)
        width = 2 * ROWS if half is None else ROWS
        with jax.named_scope("attend"):
            return call(
                functools.partial(attend, distance, first, half),
                jax.ShapeDtypeStruct((4, STATE, width), jnp.float32),
                [smem] + [vmem] * (len(operands) - 1),
                flops=16 * HD * ROWS * width * 4 * count,
                moved=8 * 2**20,
                input_output_aliases={} if first or half is not None else {len(operands) - 1: 0},
            )(*operands)

    state = step([pairs], 0, None)
    for distance in range(1, 4):
        first_chain, state = lax.optimization_barrier((first_chain, state))
        second_chain, state = lax.optimization_barrier((second_chain, state))
        arrived = [first_chain, second_chain]
        first_chain = hop(first_chain)
        if distance < 3:
            second_chain = hop(second_chain)
        state = step(arrived, distance, state)
    theirs = step([first_chain], 4, state, 1)
    with jax.named_scope("swap_terms"):
        theirs = swap(theirs)
    mine = step([first_chain], 4, state, 0)
    with jax.named_scope("join"):
        attended = call(
            join,
            jax.ShapeDtypeStruct((heads, SLICE, HD), bf16),
            [smem, vmem, vmem],
        )(lengths, mine, theirs)
    with jax.named_scope("heads_to_tokens"):
        attended = lax.all_to_all(attended, ("y", "x"), 0, 0, tiled=True)
    with jax.named_scope("unpack"):
        out = call(unpack, jax.ShapeDtypeStruct((SLICE, heads * HD), bf16), [vmem])(attended)
    return out[None]


def solution(mesh):
    fine = Mesh(mesh.devices.reshape(2, 4, 2, 4, 4), ("zlo", "y", "core", "x", "zhi"))
    span, seq = ("zlo", "y", "core"), ("x", "zhi")
    return jax.shard_map(
        shards,
        mesh=fine,
        in_specs=(P(None, span, seq, None), P()),
        out_specs=P(span, seq, None),
        check_vma=False,
    )
```

```python
import functools
import math

import jax
import jax.numpy as jnp
from jax import lax
from jax.experimental import pallas as pl
from jax.experimental.pallas import tpu as pltpu
from jax.sharding import Mesh
from jax.sharding import PartitionSpec as P

HD = 128
SLICE = 64
ROWS = 256
FILL = -1e30
STATE = HD + 16
SCALE = math.log2(math.e) / math.sqrt(HD)
VMEM = pltpu.VMEM
RING = ("zlo", "core", "zhi")


def pack(qkv_ref, out_ref):
    for head in range(out_ref.shape[0]):
        columns = slice(head * HD, (head + 1) * HD)
        for part in range(3):
            out_ref[head, part * SLICE : (part + 1) * SLICE] = qkv_ref[part, :, columns]


def unpack(parts_ref, out_ref):
    for head in range(parts_ref.shape[0]):
        out_ref[:, head * HD : (head + 1) * HD] = parts_ref[head]


def split(parts_ref, query_ref, pair_ref):
    for span in range(4):
        block = parts_ref.at[4 * span : 4 * span + 4]
        query_ref[span] = block[:, :SLICE, :].reshape(ROWS, HD)
        pair_ref[span, :ROWS] = block[:, SLICE : 2 * SLICE, :].reshape(ROWS, HD)
        turned = block[:, 2 * SLICE :, :].reshape(ROWS, HD).T
        pair_ref[span, ROWS : ROWS + HD] = turned[:, :HD]
        pair_ref[span, ROWS + HD :] = turned[:, HD:]


def attend(distance, first, half, *refs):
    refs = list(refs)
    lengths_ref, own_ref, other_ref = refs[:3]
    arrivals = refs[3:-1] if first else refs[3:-2]
    before_ref = None if first else refs[-2]
    state_ref = refs[-1]
    core = lax.axis_index("core")
    zlo = lax.axis_index("zlo")
    zed = lax.axis_index("zhi") * 2 + zlo
    pieces = [(span, number) for span in range(4) for number in range(len(arrivals))]
    source_zed = lax.rem(zed + 8 + jnp.where(core == 0, -distance, distance), 8)
    source_zlo = lax.rem(source_zed, 2)
    source_core = [core, 1 - core]
    offset = (source_zed // 2) * SLICE
    aligned = distance % 2 == 0

    width = state_ref.shape[2]
    columns = slice(ROWS if half == 1 else 0, ROWS if half == 0 else 2 * ROWS)

    ones = jnp.where(lax.broadcasted_iota(jnp.int32, (16, ROWS), 0) < 8, 1.0, 0.0)
    ones = ones.astype(jnp.bfloat16)

    def scores_of(step, count, last):
        if half is None:
            queries = jnp.concatenate([own_ref[step], other_ref[step]], axis=0)
        else:
            queries = (own_ref, other_ref)[half][step]
        row = lax.broadcasted_iota(jnp.int32, (SLICE, width), 0)
        other_half = lax.broadcasted_iota(jnp.int32, (SLICE, width), 1) >= ROWS
        scores = []
        for span, number in pieces:
            if span >= count:
                continue
            score = lax.dot_general(
                arrivals[number][span, :ROWS, :],
                queries,
                (((1,), (1,)), ((), ())),
                preferred_element_type=jnp.float32,
            )
            live = lengths_ref[source_zlo * 8 + 2 * span + source_core[number]]
            for part in range(4):
                rows = score[part * SLICE : (part + 1) * SLICE]
                bound = live - part * ROWS - offset
                if span == last:
                    own_bound = jnp.where(source_core[number] <= core, bound, 0)
                    other_bound = jnp.where(source_core[number] <= 1 - core, bound, 0)
                    if half is None:
                        bound = jnp.where(other_half, other_bound, own_bound)
                    else:
                        bound = (own_bound, other_bound)[half]
                    rows = jnp.where(row < bound, rows, FILL)
                elif part >= 2:
                    rows = jnp.where(row < bound, rows, FILL)
                scores.append(rows)
        return jnp.concatenate(scores, axis=0)

    def values_of(count):
        values = []
        for span, number in pieces:
            if span < count:
                block = arrivals[number].at[span]
                turned = jnp.concatenate([block[ROWS : ROWS + HD, :], block[ROWS + HD :, :]], axis=1)
                values.append(jnp.concatenate([turned, ones], axis=0))
        return jnp.concatenate(values, axis=1)

    def add(steps):
        scores = [scores_of(*step) for step in steps]
        olds = [None if first else before_ref[step, HD + 8 : HD + 9, columns] for step, _, _ in steps]
        peaks = []
        for old, score in zip(olds, scores):
            peak = jnp.max(score, axis=0, keepdims=True)
            peaks.append(peak if first else jnp.maximum(old, peak))
        weights = []
        for (_, _, last), score, peak in zip(steps, scores, peaks):
            weight = jnp.exp2((score - peak) * SCALE)
            if last == 0:
                weight = jnp.where(score > FILL, weight, 0.0)
            weights.append(weight.astype(jnp.bfloat16))
        fresh = [
            jnp.dot(values_of(count), weight, preferred_element_type=jnp.float32)[: HD + 8]
            for (_, count, _), weight in zip(steps, weights)
        ]
        for (step, _, _), old, peak, term in zip(steps, olds, peaks, fresh):
            if not first:
                keep = jnp.exp2((old - peak) * SCALE)
                term = before_ref[step, : HD + 8, columns] * keep + term
            state_ref[step, : HD + 8, :] = term
            state_ref[step, HD + 8 :, :] = jnp.broadcast_to(peak, (8, width))

    if aligned:
        add([(step, step + 1, step) for step in range(4)])
    else:

        @pl.when(source_zlo < zlo)
        def _():
            @pl.loop(0, 2)
            def _(pair):
                add([(2 * pair, 4, -1), (2 * pair + 1, 4, -1)])

        @pl.when(source_zlo > zlo)
        def _():
            state_ref[...] = before_ref[...]


def join(lengths_ref, own_ref, other_ref, out_ref):
    core = lax.axis_index("core")
    zlo = lax.axis_index("zlo")
    offset = lax.axis_index("zhi") * SLICE
    for step in range(4):
        live = lengths_ref[zlo * 8 + 2 * step + core]
        first_peak = own_ref[step, HD + 8 : HD + 9, :]
        second_peak = other_ref[step, HD + 8 : HD + 9, :]
        peak = jnp.maximum(first_peak, second_peak)
        first = jnp.exp2((first_peak - peak) * SCALE)
        second = jnp.exp2((second_peak - peak) * SCALE)
        total = own_ref[step, HD : HD + 1, :] * first + other_ref[step, HD : HD + 1, :] * second
        numerator = own_ref[step, :HD, :] * first + other_ref[step, :HD, :] * second
        result = (numerator / total).T
        row = lax.broadcasted_iota(jnp.int32, (SLICE, HD), 0)
        for piece in range(4):
            part = result[piece * SLICE : (piece + 1) * SLICE]
            part = jnp.where(row < live - piece * ROWS - offset, part, 0.0)
            out_ref[4 * step + piece] = part.astype(jnp.bfloat16)


def call(kernel, out_shape, in_specs, flops=0, moved=0, **kw):
    spec = pl.BlockSpec(memory_space=VMEM)
    return pl.pallas_call(
        kernel,
        out_shape=out_shape,
        in_specs=in_specs,
        out_specs=jax.tree.map(lambda _: spec, out_shape),
        compiler_params=pltpu.CompilerParams(vmem_limit_bytes=40 * 2**20),
        cost_estimate=pl.CostEstimate(flops=flops, bytes_accessed=moved, transcendentals=0),
        **kw,
    )


def shards(qkv, lengths):
    vmem = pl.BlockSpec(memory_space=VMEM)
    smem = pl.BlockSpec(memory_space=pltpu.SMEM)
    heads = 16
    bf16 = jnp.bfloat16
    with jax.named_scope("pack"):
        parts = call(pack, jax.ShapeDtypeStruct((heads, 3 * SLICE, HD), bf16), [vmem])(qkv[:, 0])
    with jax.named_scope("tokens_to_heads"):
        parts = lax.all_to_all(parts, ("y", "x"), 0, 0, tiled=True)
    with jax.named_scope("split"):
        own, pairs = call(
            split,
            [
                jax.ShapeDtypeStruct((4, ROWS, HD), bf16),
                jax.ShapeDtypeStruct((4, 2 * ROWS, HD), bf16),
            ],
            [vmem],
        )(parts)

    chips = 8
    place = [z % 2 * 8 + z // 2 for z in range(chips)]
    route = [(place[z], place[(z + 1) % chips]) for z in range(chips)]
    route += [(place[z] + 4, place[(z - 1) % chips] + 4) for z in range(chips)]

    def hop(block):
        with jax.named_scope("ring"):
            return lax.ppermute(block, RING, route)

    def swap(block):
        return lax.ppermute(block, "core", [(0, 1), (1, 0)])

    first_chain = hop(pairs)
    with jax.named_scope("swap_queries"):
        other = swap(own)
    with jax.named_scope("swap_pairs"):
        second = swap(pairs)
    other, second = lax.optimization_barrier((other, second))
    second_chain = hop(second)

    def step(arrivals, distance, state, half=None):
        first = state is None
        operands = [lengths, own, other] + arrivals + ([] if first else [state])
        count = 4 * len(arrivals)
        width = 2 * ROWS if half is None else ROWS
        with jax.named_scope("attend"):
            return call(
                functools.partial(attend, distance, first, half),
                jax.ShapeDtypeStruct((4, STATE, width), jnp.float32),
                [smem] + [vmem] * (len(operands) - 1),
                flops=16 * HD * ROWS * width * 4 * count,
                moved=8 * 2**20,
                input_output_aliases={} if first or half is not None else {len(operands) - 1: 0},
            )(*operands)

    state = step([pairs], 0, None)
    for distance in range(1, 4):
        first_chain, state = lax.optimization_barrier((first_chain, state))
        second_chain, state = lax.optimization_barrier((second_chain, state))
        arrived = [first_chain, second_chain]
        first_chain = hop(first_chain)
        if distance < 3:
            second_chain = hop(second_chain)
        state = step(arrived, distance, state)
    theirs = step([first_chain], 4, state, 1)
    with jax.named_scope("swap_terms"):
        theirs = swap(theirs)
    mine = step([first_chain], 4, state, 0)
    with jax.named_scope("join"):
        attended = call(
            join,
            jax.ShapeDtypeStruct((heads, SLICE, HD), bf16),
            [smem, vmem, vmem],
        )(lengths, mine, theirs)
    with jax.named_scope("heads_to_tokens"):
        attended = lax.all_to_all(attended, ("y", "x"), 0, 0, tiled=True)
    with jax.named_scope("unpack"):
        out = call(unpack, jax.ShapeDtypeStruct((SLICE, heads * HD), bf16), [vmem])(attended)
    return out[None]


def solution(mesh):
    fine = Mesh(mesh.devices.reshape(2, 4, 2, 4, 4), ("zlo", "y", "core", "x", "zhi"))
    span, seq = ("zlo", "y", "core"), ("x", "zhi")
    return jax.shard_map(
        shards,
        mesh=fine,
        in_specs=(P(None, span, seq, None), P()),
        out_specs=P(span, seq, None),
        check_vma=False,
    )
```

```python
import functools
import math

import jax
import jax.numpy as jnp
from jax import lax
from jax.experimental import pallas as pl
from jax.experimental.pallas import tpu as pltpu
from jax.sharding import Mesh
from jax.sharding import PartitionSpec as P

HD = 128
SLICE = 64
ROWS = 256
FILL = -1e30
STATE = HD + 16
SCALE = math.log2(math.e) / math.sqrt(HD)
VMEM = pltpu.VMEM
RING = ("zlo", "core", "zhi")


def pack(qkv_ref, out_ref):
    for head in range(out_ref.shape[0]):
        columns = slice(head * HD, (head + 1) * HD)
        for part in range(3):
            out_ref[head, part * SLICE : (part + 1) * SLICE] = qkv_ref[part, :, columns]


def unpack(parts_ref, out_ref):
    for head in range(parts_ref.shape[0]):
        out_ref[:, head * HD : (head + 1) * HD] = parts_ref[head]


def split(parts_ref, query_ref, pair_ref):
    for span in range(4):
        block = parts_ref.at[4 * span : 4 * span + 4]
        query_ref[span] = block[:, :SLICE, :].reshape(ROWS, HD)
        pair_ref[span, :ROWS] = block[:, SLICE : 2 * SLICE, :].reshape(ROWS, HD)
        turned = block[:, 2 * SLICE :, :].reshape(ROWS, HD).T
        pair_ref[span, ROWS : ROWS + HD] = turned[:, :HD]
        pair_ref[span, ROWS + HD :] = turned[:, HD:]


def attend(distance, chains, first, half, *refs):
    refs = list(refs)
    lengths_ref, own_ref, other_ref = refs[:3]
    arrivals = refs[3:-1] if first else refs[3:-2]
    before_ref = None if first else refs[-2]
    state_ref = refs[-1]
    core = lax.axis_index("core")
    zlo = lax.axis_index("zlo")
    zed = lax.axis_index("zhi") * 2 + zlo
    pieces = [(span, number) for span in range(4) for number in range(len(arrivals))]
    source_zed = lax.rem(zed + 8 + jnp.where(core == 0, -distance, distance), 8)
    source_zlo = lax.rem(source_zed, 2)
    source_core = [core if chain == 0 else 1 - core for chain in chains]
    offset = (source_zed // 2) * SLICE
    aligned = distance % 2 == 0

    width = state_ref.shape[2]
    columns = slice(ROWS if half == 1 else 0, ROWS if half == 0 else 2 * ROWS)

    ones = jnp.where(lax.broadcasted_iota(jnp.int32, (16, ROWS), 0) < 8, 1.0, 0.0)
    ones = ones.astype(jnp.bfloat16)

    def scores_of(step, count, last):
        if half is None:
            queries = jnp.concatenate([own_ref[step], other_ref[step]], axis=0)
        else:
            queries = (own_ref, other_ref)[half][step]
        row = lax.broadcasted_iota(jnp.int32, (SLICE, width), 0)
        other_half = lax.broadcasted_iota(jnp.int32, (SLICE, width), 1) >= ROWS
        scores = []
        for span, number in pieces:
            if span >= count:
                continue
            score = lax.dot_general(
                arrivals[number][span, :ROWS, :],
                queries,
                (((1,), (1,)), ((), ())),
                preferred_element_type=jnp.float32,
            )
            live = lengths_ref[source_zlo * 8 + 2 * span + source_core[number]]
            for part in range(4):
                rows = score[part * SLICE : (part + 1) * SLICE]
                bound = live - part * ROWS - offset
                if span == last:
                    own_bound = jnp.where(source_core[number] <= core, bound, 0)
                    other_bound = jnp.where(source_core[number] <= 1 - core, bound, 0)
                    if half is None:
                        bound = jnp.where(other_half, other_bound, own_bound)
                    else:
                        bound = (own_bound, other_bound)[half]
                    rows = jnp.where(row < bound, rows, FILL)
                elif part >= 2:
                    rows = jnp.where(row < bound, rows, FILL)
                scores.append(rows)
        return jnp.concatenate(scores, axis=0)

    def values_of(count):
        values = []
        for span, number in pieces:
            if span < count:
                block = arrivals[number].at[span]
                turned = jnp.concatenate([block[ROWS : ROWS + HD, :], block[ROWS + HD :, :]], axis=1)
                values.append(jnp.concatenate([turned, ones], axis=0))
        return jnp.concatenate(values, axis=1)

    def add(steps):
        scores = [scores_of(*step) for step in steps]
        olds = [None if first else before_ref[step, HD + 8 : HD + 9, columns] for step, _, _ in steps]
        peaks = []
        for old, score in zip(olds, scores):
            peak = jnp.max(score, axis=0, keepdims=True)
            peaks.append(peak if first else jnp.maximum(old, peak))
        weights = []
        for (_, _, last), score, peak in zip(steps, scores, peaks):
            weight = jnp.exp2((score - peak) * SCALE)
            if last == 0:
                weight = jnp.where(score > FILL, weight, 0.0)
            weights.append(weight.astype(jnp.bfloat16))
        fresh = [
            jnp.dot(values_of(count), weight, preferred_element_type=jnp.float32)[: HD + 8]
            for (_, count, _), weight in zip(steps, weights)
        ]
        for (step, _, _), old, peak, term in zip(steps, olds, peaks, fresh):
            if not first:
                keep = jnp.exp2((old - peak) * SCALE)
                term = before_ref[step, : HD + 8, columns] * keep + term
            state_ref[step, : HD + 8, :] = term
            state_ref[step, HD + 8 :, :] = jnp.broadcast_to(peak, (8, width))

    if aligned:
        add([(step, step + 1, step) for step in range(4)])
    else:

        @pl.when(source_zlo < zlo)
        def _():
            together = 4 // len(arrivals)

            @pl.loop(0, len(arrivals))
            def _(group):
                add([(together * group + member, 4, -1) for member in range(together)])

        @pl.when(source_zlo > zlo)
        def _():
            state_ref[...] = before_ref[...]


def join(lengths_ref, own_ref, other_ref, out_ref):
    core = lax.axis_index("core")
    zlo = lax.axis_index("zlo")
    offset = lax.axis_index("zhi") * SLICE
    for step in range(4):
        live = lengths_ref[zlo * 8 + 2 * step + core]
        first_peak = own_ref[step, HD + 8 : HD + 9, :]
        second_peak = other_ref[step, HD + 8 : HD + 9, :]
        peak = jnp.maximum(first_peak, second_peak)
        first = jnp.exp2((first_peak - peak) * SCALE)
        second = jnp.exp2((second_peak - peak) * SCALE)
        total = own_ref[step, HD : HD + 1, :] * first + other_ref[step, HD : HD + 1, :] * second
        numerator = own_ref[step, :HD, :] * first + other_ref[step, :HD, :] * second
        result = (numerator / total).T
        row = lax.broadcasted_iota(jnp.int32, (SLICE, HD), 0)
        for piece in range(4):
            part = result[piece * SLICE : (piece + 1) * SLICE]
            part = jnp.where(row < live - piece * ROWS - offset, part, 0.0)
            out_ref[4 * step + piece] = part.astype(jnp.bfloat16)


def call(kernel, out_shape, in_specs, flops=0, moved=0, **kw):
    spec = pl.BlockSpec(memory_space=VMEM)
    return pl.pallas_call(
        kernel,
        out_shape=out_shape,
        in_specs=in_specs,
        out_specs=jax.tree.map(lambda _: spec, out_shape),
        compiler_params=pltpu.CompilerParams(vmem_limit_bytes=40 * 2**20),
        cost_estimate=pl.CostEstimate(flops=flops, bytes_accessed=moved, transcendentals=0),
        **kw,
    )


def shards(qkv, lengths):
    vmem = pl.BlockSpec(memory_space=VMEM)
    smem = pl.BlockSpec(memory_space=pltpu.SMEM)
    heads = 16
    bf16 = jnp.bfloat16
    with jax.named_scope("pack"):
        parts = call(pack, jax.ShapeDtypeStruct((heads, 3 * SLICE, HD), bf16), [vmem])(qkv[:, 0])
    with jax.named_scope("tokens_to_heads"):
        parts = lax.all_to_all(parts, ("y", "x"), 0, 0, tiled=True)
    with jax.named_scope("split"):
        own, pairs = call(
            split,
            [
                jax.ShapeDtypeStruct((4, ROWS, HD), bf16),
                jax.ShapeDtypeStruct((4, 2 * ROWS, HD), bf16),
            ],
            [vmem],
        )(parts)

    chips = 8
    place = [z % 2 * 8 + z // 2 for z in range(chips)]
    route = [(place[z], place[(z + 1) % chips]) for z in range(chips)]
    route += [(place[z] + 4, place[(z - 1) % chips] + 4) for z in range(chips)]

    def hop(block):
        with jax.named_scope("ring"):
            return lax.ppermute(block, RING, route)

    def swap(block):
        return lax.ppermute(block, "core", [(0, 1), (1, 0)])

    first_chain = hop(pairs)
    with jax.named_scope("swap_queries"):
        other = swap(own)
    with jax.named_scope("swap_pairs"):
        second = swap(pairs)
    other, second = lax.optimization_barrier((other, second))
    second_chain = hop(second)

    def step(arrivals, distance, state, half=None, chains=(0, 1)):
        first = state is None
        operands = [lengths, own, other] + arrivals + ([] if first else [state])
        count = 4 * len(arrivals)
        width = 2 * ROWS if half is None else ROWS
        with jax.named_scope("attend"):
            return call(
                functools.partial(attend, distance, chains[: len(arrivals)], first, half),
                jax.ShapeDtypeStruct((4, STATE, width), jnp.float32),
                [smem] + [vmem] * (len(operands) - 1),
                flops=16 * HD * ROWS * width * 4 * count,
                moved=8 * 2**20,
                input_output_aliases={} if first or half is not None else {len(operands) - 1: 0},
            )(*operands)

    state = step([pairs], 0, None)
    def after(block, state):
        return lax.optimization_barrier((block, state))

    for distance in range(1, 3):
        first_chain, state = after(first_chain, state)
        second_chain, state = after(second_chain, state)
        arrived = [first_chain, second_chain]
        first_chain, second_chain = hop(first_chain), hop(second_chain)
        state = step(arrived, distance, state)
    arrived, state = after(first_chain, state)
    first_chain = hop(arrived)
    state = step([arrived], 3, state)
    second_chain, state = after(second_chain, state)
    state = step([second_chain], 3, state, chains=(1,))
    theirs = step([first_chain], 4, state, 1)
    with jax.named_scope("swap_terms"):
        theirs = swap(theirs)
    mine = step([first_chain], 4, state, 0)
    with jax.named_scope("join"):
        attended = call(
            join,
            jax.ShapeDtypeStruct((heads, SLICE, HD), bf16),
            [smem, vmem, vmem],
        )(lengths, mine, theirs)
    with jax.named_scope("heads_to_tokens"):
        attended = lax.all_to_all(attended, ("y", "x"), 0, 0, tiled=True)
    with jax.named_scope("unpack"):
        out = call(unpack, jax.ShapeDtypeStruct((SLICE, heads * HD), bf16), [vmem])(attended)
    return out[None]


def solution(mesh):
    fine = Mesh(mesh.devices.reshape(2, 4, 2, 4, 4), ("zlo", "y", "core", "x", "zhi"))
    span, seq = ("zlo", "y", "core"), ("x", "zhi")
    return jax.shard_map(
        shards,
        mesh=fine,
        in_specs=(P(None, span, seq, None), P()),
        out_specs=P(span, seq, None),
        check_vma=False,
    )
```

```python
import functools
import math

import jax
import jax.numpy as jnp
from jax import lax
from jax.experimental import pallas as pl
from jax.experimental.pallas import tpu as pltpu
from jax.sharding import Mesh
from jax.sharding import PartitionSpec as P

HD = 128
SLICE = 64
ROWS = 256
FILL = -1e30
STATE = HD + 16
SCALE = math.log2(math.e) / math.sqrt(HD)
VMEM = pltpu.VMEM
RING = ("zlo", "core", "zhi")


def pack(qkv_ref, out_ref):
    for head in range(out_ref.shape[0]):
        columns = slice(head * HD, (head + 1) * HD)
        for part in range(3):
            out_ref[head, part * SLICE : (part + 1) * SLICE] = qkv_ref[part, :, columns]


def unpack(parts_ref, out_ref):
    for head in range(parts_ref.shape[0]):
        out_ref[:, head * HD : (head + 1) * HD] = parts_ref[head]


def split(parts_ref, query_ref, pair_ref):
    for span in range(4):
        block = parts_ref.at[4 * span : 4 * span + 4]
        query_ref[span] = block[:, :SLICE, :].reshape(ROWS, HD)
        pair_ref[span, :ROWS] = block[:, SLICE : 2 * SLICE, :].reshape(ROWS, HD)
        turned = block[:, 2 * SLICE :, :].reshape(ROWS, HD).T
        pair_ref[span, ROWS : ROWS + HD] = turned[:, :HD]
        pair_ref[span, ROWS + HD :] = turned[:, HD:]


def attend(distance, chains, begin, steps, first, half, *refs):
    refs = list(refs)
    lengths_ref, own_ref, other_ref = refs[:3]
    arrivals = refs[3:-1] if first else refs[3:-2]
    before_ref = None if first else refs[-2]
    state_ref = refs[-1]
    core = lax.axis_index("core")
    zlo = lax.axis_index("zlo")
    zed = lax.axis_index("zhi") * 2 + zlo
    end = begin + arrivals[0].shape[0]
    pieces = [(span, number) for span in range(begin, end) for number in range(len(arrivals))]
    source_zed = lax.rem(zed + 8 + jnp.where(core == 0, -distance, distance), 8)
    source_zlo = lax.rem(source_zed, 2)
    source_core = [core if chain == 0 else 1 - core for chain in chains]
    offset = (source_zed // 2) * SLICE
    aligned = distance % 2 == 0

    width = state_ref.shape[2]
    columns = slice(ROWS if half == 1 else 0, ROWS if half == 0 else 2 * ROWS)

    ones = jnp.where(lax.broadcasted_iota(jnp.int32, (16, ROWS), 0) < 8, 1.0, 0.0)
    ones = ones.astype(jnp.bfloat16)

    def scores_of(step, count, last):
        if half is None:
            queries = jnp.concatenate([own_ref[step], other_ref[step]], axis=0)
        else:
            queries = (own_ref, other_ref)[half][step]
        row = lax.broadcasted_iota(jnp.int32, (SLICE, width), 0)
        other_half = lax.broadcasted_iota(jnp.int32, (SLICE, width), 1) >= ROWS
        scores = []
        for span, number in pieces:
            if span >= count:
                continue
            score = lax.dot_general(
                arrivals[number][span - begin, :ROWS, :],
                queries,
                (((1,), (1,)), ((), ())),
                preferred_element_type=jnp.float32,
            )
            live = lengths_ref[source_zlo * 8 + 2 * span + source_core[number]]
            for part in range(4):
                rows = score[part * SLICE : (part + 1) * SLICE]
                bound = live - part * ROWS - offset
                if span == last:
                    own_bound = jnp.where(source_core[number] <= core, bound, 0)
                    other_bound = jnp.where(source_core[number] <= 1 - core, bound, 0)
                    if half is None:
                        bound = jnp.where(other_half, other_bound, own_bound)
                    else:
                        bound = (own_bound, other_bound)[half]
                    rows = jnp.where(row < bound, rows, FILL)
                elif part >= 2:
                    rows = jnp.where(row < bound, rows, FILL)
                scores.append(rows)
        return jnp.concatenate(scores, axis=0)

    def values_of(count):
        values = []
        for span, number in pieces:
            if span < count:
                block = arrivals[number].at[span - begin]
                turned = jnp.concatenate([block[ROWS : ROWS + HD, :], block[ROWS + HD :, :]], axis=1)
                values.append(jnp.concatenate([turned, ones], axis=0))
        return jnp.concatenate(values, axis=1)

    def add(work):
        scores = [scores_of(*step) for step in work]
        olds = [None if first else before_ref[step, HD + 8 : HD + 9, columns] for step, _, _ in work]
        peaks = []
        for old, score in zip(olds, scores):
            peak = jnp.max(score, axis=0, keepdims=True)
            peaks.append(peak if first else jnp.maximum(old, peak))
        weights = []
        for (_, _, last), score, peak in zip(work, scores, peaks):
            weight = jnp.exp2((score - peak) * SCALE)
            if last == 0:
                weight = jnp.where(score > FILL, weight, 0.0)
            weights.append(weight.astype(jnp.bfloat16))
        fresh = [
            jnp.dot(values_of(count), weight, preferred_element_type=jnp.float32)[: HD + 8]
            for (_, count, _), weight in zip(work, weights)
        ]
        for (step, _, _), old, peak, term in zip(work, olds, peaks, fresh):
            if not first:
                keep = jnp.exp2((old - peak) * SCALE)
                term = before_ref[step, : HD + 8, columns] * keep + term
            place = step - steps[0]
            state_ref[place, : HD + 8, :] = term
            state_ref[place, HD + 8 :, :] = jnp.broadcast_to(peak, (8, width))

    if aligned:
        add([(step, step + 1, step) for step in steps])
    else:

        @pl.when(source_zlo < zlo)
        def _():
            together = 4 // len(arrivals)

            @pl.loop(0, len(arrivals))
            def _(group):
                add([(together * group + member, 4, -1) for member in range(together)])

        @pl.when(source_zlo > zlo)
        def _():
            state_ref[...] = before_ref[...]


def join(lengths_ref, state_ref, mine_ref, early_ref, late_ref, out_ref):
    core = lax.axis_index("core")
    zlo = lax.axis_index("zlo")
    offset = lax.axis_index("zhi") * SLICE
    for step in range(4):
        live = lengths_ref[zlo * 8 + 2 * step + core]
        own = state_ref.at[step] if step < 2 else mine_ref.at[step - 2]
        other = early_ref.at[step] if step < 2 else late_ref.at[step - 2]
        first_peak = own[HD + 8 : HD + 9, :ROWS]
        second_peak = other[HD + 8 : HD + 9, :]
        peak = jnp.maximum(first_peak, second_peak)
        first = jnp.exp2((first_peak - peak) * SCALE)
        second = jnp.exp2((second_peak - peak) * SCALE)
        total = own[HD : HD + 1, :ROWS] * first + other[HD : HD + 1, :] * second
        numerator = own[:HD, :ROWS] * first + other[:HD, :] * second
        result = (numerator / total).T
        row = lax.broadcasted_iota(jnp.int32, (SLICE, HD), 0)
        for piece in range(4):
            part = result[piece * SLICE : (piece + 1) * SLICE]
            part = jnp.where(row < live - piece * ROWS - offset, part, 0.0)
            out_ref[4 * step + piece] = part.astype(jnp.bfloat16)


def call(kernel, out_shape, in_specs, flops=0, moved=0, **kw):
    spec = pl.BlockSpec(memory_space=VMEM)
    return pl.pallas_call(
        kernel,
        out_shape=out_shape,
        in_specs=in_specs,
        out_specs=jax.tree.map(lambda _: spec, out_shape),
        compiler_params=pltpu.CompilerParams(vmem_limit_bytes=40 * 2**20),
        cost_estimate=pl.CostEstimate(flops=flops, bytes_accessed=moved, transcendentals=0),
        **kw,
    )


def shards(qkv, lengths):
    vmem = pl.BlockSpec(memory_space=VMEM)
    smem = pl.BlockSpec(memory_space=pltpu.SMEM)
    heads = 16
    bf16 = jnp.bfloat16
    with jax.named_scope("pack"):
        parts = call(pack, jax.ShapeDtypeStruct((heads, 3 * SLICE, HD), bf16), [vmem])(qkv[:, 0])
    with jax.named_scope("tokens_to_heads"):
        parts = lax.all_to_all(parts, ("y", "x"), 0, 0, tiled=True)
    with jax.named_scope("split"):
        own, pairs = call(
            split,
            [
                jax.ShapeDtypeStruct((4, ROWS, HD), bf16),
                jax.ShapeDtypeStruct((4, 2 * ROWS, HD), bf16),
            ],
            [vmem],
        )(parts)

    chips = 8
    place = [z % 2 * 8 + z // 2 for z in range(chips)]
    route = [(place[z], place[(z + 1) % chips]) for z in range(chips)]
    route += [(place[z] + 4, place[(z - 1) % chips] + 4) for z in range(chips)]

    def hop(block):
        with jax.named_scope("ring"):
            return lax.ppermute(block, RING, route)

    def swap(block):
        return lax.ppermute(block, "core", [(0, 1), (1, 0)])

    first_chain = hop(pairs)
    with jax.named_scope("swap_queries"):
        other = swap(own)
    with jax.named_scope("swap_pairs"):
        second = swap(pairs)
    other, second = lax.optimization_barrier((other, second))
    second_chain = hop(second)

    def step(arrivals, distance, state, half=None, chains=(0, 1), begin=0, steps=(0, 1, 2, 3)):
        first = state is None
        operands = [lengths, own, other] + arrivals + ([] if first else [state])
        count = sum(a.shape[0] for a in arrivals)
        width = 2 * ROWS if half is None else ROWS
        kernel = functools.partial(
            attend, distance, chains[: len(arrivals)], begin, steps, first, half
        )
        with jax.named_scope("attend"):
            return call(
                kernel,
                jax.ShapeDtypeStruct((len(steps), STATE, width), jnp.float32),
                [smem] + [vmem] * (len(operands) - 1),
                flops=4 * HD * ROWS * width * len(steps) * 4 * count,
                moved=8 * 2**20,
                input_output_aliases={} if first or half is not None else {len(operands) - 1: 0},
            )(*operands)

    state = step([pairs], 0, None)
    def after(block, state):
        return lax.optimization_barrier((block, state))

    for distance in range(1, 3):
        first_chain, state = after(first_chain, state)
        second_chain, state = after(second_chain, state)
        arrived = [first_chain, second_chain]
        first_chain, second_chain = hop(first_chain), hop(second_chain)
        state = step(arrived, distance, state)
    arrived, state = after(first_chain, state)
    halves = [hop(arrived[:2]), hop(arrived[2:])]
    state = step([arrived], 3, state)
    second_chain, state = after(second_chain, state)
    state = step([second_chain], 3, state, chains=(1,))
    block, state = after(halves[0], state)
    state = step([block], 4, state)
    with jax.named_scope("swap_terms"):
        early = swap(state[:2, :, ROWS:])
    block, state, early = lax.optimization_barrier((halves[1], state, early))
    late = step([block], 4, state, 1, begin=2, steps=(2, 3))
    with jax.named_scope("swap_terms"):
        late = swap(late)
    mine = step([block], 4, state, 0, begin=2, steps=(2, 3))
    with jax.named_scope("join"):
        attended = call(
            join,
            jax.ShapeDtypeStruct((heads, SLICE, HD), bf16),
            [smem, vmem, vmem, vmem, vmem],
        )(lengths, state, mine, early, late)
    with jax.named_scope("heads_to_tokens"):
        attended = lax.all_to_all(attended, ("y", "x"), 0, 0, tiled=True)
    with jax.named_scope("unpack"):
        out = call(unpack, jax.ShapeDtypeStruct((SLICE, heads * HD), bf16), [vmem])(attended)
    return out[None]


def solution(mesh):
    fine = Mesh(mesh.devices.reshape(2, 4, 2, 4, 4), ("zlo", "y", "core", "x", "zhi"))
    span, seq = ("zlo", "y", "core"), ("x", "zhi")
    return jax.shard_map(
        shards,
        mesh=fine,
        in_specs=(P(None, span, seq, None), P()),
        out_specs=P(span, seq, None),
        check_vma=False,
    )
```

```python
import functools
import math

import jax
import jax.numpy as jnp
from jax import lax
from jax.experimental import pallas as pl
from jax.experimental.pallas import tpu as pltpu
from jax.sharding import Mesh
from jax.sharding import PartitionSpec as P

HD = 128
SLICE = 64
ROWS = 256
FILL = -1e30
STATE = HD + 16
SCALE = math.log2(math.e) / math.sqrt(HD)
VMEM = pltpu.VMEM
RING = ("zlo", "core", "zhi")


def pack(qkv_ref, out_ref):
    for head in range(out_ref.shape[0]):
        columns = slice(head * HD, (head + 1) * HD)
        for part in range(3):
            out_ref[head, part * SLICE : (part + 1) * SLICE] = qkv_ref[part, :, columns]


def unpack(parts_ref, out_ref):
    for head in range(parts_ref.shape[0]):
        out_ref[:, head * HD : (head + 1) * HD] = parts_ref[head]


def split(parts_ref, query_ref, pair_ref):
    for span in range(4):
        block = parts_ref.at[4 * span : 4 * span + 4]
        query_ref[span] = block[:, :SLICE, :].reshape(ROWS, HD)
        pair_ref[span, :ROWS] = block[:, SLICE : 2 * SLICE, :].reshape(ROWS, HD)
        turned = block[:, 2 * SLICE :, :].reshape(ROWS, HD).T
        pair_ref[span, ROWS : ROWS + HD] = turned[:, :HD]
        pair_ref[span, ROWS + HD :] = turned[:, HD:]


def attend(distance, chains, begin, steps, first, half, *refs):
    refs = list(refs)
    lengths_ref, own_ref, other_ref = refs[:3]
    arrivals = refs[3:-1] if first else refs[3:-2]
    before_ref = None if first else refs[-2]
    state_ref = refs[-1]
    core = lax.axis_index("core")
    zlo = lax.axis_index("zlo")
    zed = lax.axis_index("zhi") * 2 + zlo
    end = begin + arrivals[0].shape[0]
    pieces = [(span, number) for span in range(begin, end) for number in range(len(arrivals))]
    source_zed = lax.rem(zed + 8 + jnp.where(core == 0, -distance, distance), 8)
    source_zlo = lax.rem(source_zed, 2)
    source_core = [core if chain == 0 else 1 - core for chain in chains]
    offset = (source_zed // 2) * SLICE
    aligned = distance % 2 == 0

    width = state_ref.shape[2]
    columns = slice(ROWS if half == 1 else 0, ROWS if half == 0 else 2 * ROWS)

    ones = jnp.where(lax.broadcasted_iota(jnp.int32, (16, ROWS), 0) < 8, 1.0, 0.0)
    ones = ones.astype(jnp.bfloat16)

    def scores_of(step, count, last):
        if half is None:
            queries = jnp.concatenate([own_ref[step], other_ref[step]], axis=0)
        else:
            queries = (own_ref, other_ref)[half][step]
        row = lax.broadcasted_iota(jnp.int32, (SLICE, width), 0)
        other_half = lax.broadcasted_iota(jnp.int32, (SLICE, width), 1) >= ROWS
        scores = []
        for span, number in pieces:
            if span >= count:
                continue
            score = lax.dot_general(
                arrivals[number][span - begin, :ROWS, :],
                queries,
                (((1,), (1,)), ((), ())),
                preferred_element_type=jnp.float32,
            )
            live = lengths_ref[source_zlo * 8 + 2 * span + source_core[number]]
            for part in range(4):
                rows = score[part * SLICE : (part + 1) * SLICE]
                bound = live - part * ROWS - offset
                if span == last:
                    own_bound = jnp.where(source_core[number] <= core, bound, 0)
                    other_bound = jnp.where(source_core[number] <= 1 - core, bound, 0)
                    if half is None:
                        bound = jnp.where(other_half, other_bound, own_bound)
                    else:
                        bound = (own_bound, other_bound)[half]
                    rows = jnp.where(row < bound, rows, FILL)
                elif part >= 2:
                    rows = jnp.where(row < bound, rows, FILL)
                scores.append(rows)
        return jnp.concatenate(scores, axis=0)

    def values_of(count):
        values = []
        for span, number in pieces:
            if span < count:
                block = arrivals[number].at[span - begin]
                turned = jnp.concatenate([block[ROWS : ROWS + HD, :], block[ROWS + HD :, :]], axis=1)
                values.append(jnp.concatenate([turned, ones], axis=0))
        return jnp.concatenate(values, axis=1)

    def add(work):
        scores = [scores_of(*step) for step in work]
        olds = [None if first else before_ref[step, HD + 8 : HD + 9, columns] for step, _, _ in work]
        peaks = []
        for old, score in zip(olds, scores):
            peak = jnp.max(score, axis=0, keepdims=True)
            peaks.append(peak if first else jnp.maximum(old, peak))
        weights = []
        for (_, _, last), score, peak in zip(work, scores, peaks):
            weight = jnp.exp2((score - peak) * SCALE)
            if last == 0:
                weight = jnp.where(score > FILL, weight, 0.0)
            weights.append(weight.astype(jnp.bfloat16))
        fresh = [
            jnp.dot(values_of(count), weight, preferred_element_type=jnp.float32)[: HD + 8]
            for (_, count, _), weight in zip(work, weights)
        ]
        for (step, _, _), old, peak, term in zip(work, olds, peaks, fresh):
            if not first:
                keep = jnp.exp2((old - peak) * SCALE)
                term = before_ref[step, : HD + 8, columns] * keep + term
            place = step - steps[0]
            state_ref[place, : HD + 8, :] = term
            state_ref[place, HD + 8 :, :] = jnp.broadcast_to(peak, (8, width))

    if aligned:
        add([(step, step + 1, step) for step in steps])
    else:

        @pl.when(source_zlo < zlo)
        def _():
            together = 4 // len(arrivals)

            @pl.loop(0, len(arrivals))
            def _(group):
                add([(together * group + member, 4, -1) for member in range(together)])

        @pl.when(source_zlo > zlo)
        def _():
            state_ref[...] = before_ref[...]


def join(lengths_ref, state_ref, mine_ref, early_ref, late_ref, out_ref):
    core = lax.axis_index("core")
    zlo = lax.axis_index("zlo")
    offset = lax.axis_index("zhi") * SLICE
    for step in range(4):
        live = lengths_ref[zlo * 8 + 2 * step + core]
        own = state_ref.at[step] if step < 2 else mine_ref.at[step - 2]
        other = early_ref.at[step] if step < 2 else late_ref.at[step - 2]
        first_peak = own[HD + 8 : HD + 9, :ROWS]
        second_peak = other[HD + 8 : HD + 9, :]
        peak = jnp.maximum(first_peak, second_peak)
        first = jnp.exp2((first_peak - peak) * SCALE)
        second = jnp.exp2((second_peak - peak) * SCALE)
        total = own[HD : HD + 1, :ROWS] * first + other[HD : HD + 1, :] * second
        numerator = own[:HD, :ROWS] * first + other[:HD, :] * second
        result = (numerator / total).T
        row = lax.broadcasted_iota(jnp.int32, (SLICE, HD), 0)
        for piece in range(4):
            part = result[piece * SLICE : (piece + 1) * SLICE]
            part = jnp.where(row < live - piece * ROWS - offset, part, 0.0)
            out_ref[4 * step + piece] = part.astype(jnp.bfloat16)


def call(kernel, out_shape, in_specs, flops=0, moved=0, **kw):
    spec = pl.BlockSpec(memory_space=VMEM)
    return pl.pallas_call(
        kernel,
        out_shape=out_shape,
        in_specs=in_specs,
        out_specs=jax.tree.map(lambda _: spec, out_shape),
        compiler_params=pltpu.CompilerParams(vmem_limit_bytes=40 * 2**20),
        cost_estimate=pl.CostEstimate(flops=flops, bytes_accessed=moved, transcendentals=0),
        **kw,
    )


def shards(qkv, lengths):
    vmem = pl.BlockSpec(memory_space=VMEM)
    smem = pl.BlockSpec(memory_space=pltpu.SMEM)
    heads = 16
    bf16 = jnp.bfloat16
    with jax.named_scope("pack"):
        parts = call(pack, jax.ShapeDtypeStruct((heads, 3 * SLICE, HD), bf16), [vmem])(qkv[:, 0])
    with jax.named_scope("tokens_to_heads"):
        parts = lax.all_to_all(parts, ("y", "x"), 0, 0, tiled=True)
    with jax.named_scope("split"):
        own, pairs = call(
            split,
            [
                jax.ShapeDtypeStruct((4, ROWS, HD), bf16),
                jax.ShapeDtypeStruct((4, 2 * ROWS, HD), bf16),
            ],
            [vmem],
        )(parts)

    chips = 8
    place = [z % 2 * 8 + z // 2 for z in range(chips)]
    route = [(place[z], place[(z + 1) % chips]) for z in range(chips)]
    route += [(place[z] + 4, place[(z - 1) % chips] + 4) for z in range(chips)]

    def hop(block):
        with jax.named_scope("ring"):
            return lax.ppermute(block, RING, route)

    def swap(block):
        return lax.ppermute(block, "core", [(0, 1), (1, 0)])

    first_chain = hop(pairs)
    with jax.named_scope("swap_queries"):
        other = swap(own)
    with jax.named_scope("swap_pairs"):
        second = swap(pairs)
    other, second = lax.optimization_barrier((other, second))
    second_chain = hop(second)

    def step(arrivals, distance, state, half=None, chains=(0, 1), begin=0, steps=(0, 1, 2, 3)):
        first = state is None
        operands = [lengths, own, other] + arrivals + ([] if first else [state])
        count = sum(a.shape[0] for a in arrivals)
        width = 2 * ROWS if half is None else ROWS
        kernel = functools.partial(
            attend, distance, chains[: len(arrivals)], begin, steps, first, half
        )
        with jax.named_scope("attend"):
            return call(
                kernel,
                jax.ShapeDtypeStruct((len(steps), STATE, width), jnp.float32),
                [smem] + [vmem] * (len(operands) - 1),
                flops=4 * HD * ROWS * width * len(steps) * 4 * count,
                moved=8 * 2**20,
                input_output_aliases={} if first or half is not None else {len(operands) - 1: 0},
            )(*operands)

    state = step([pairs], 0, None)
    def after(block, state):
        return lax.optimization_barrier((block, state))

    for distance in range(1, 3):
        first_chain, state = after(first_chain, state)
        second_chain, state = after(second_chain, state)
        arrived = [first_chain, second_chain]
        first_chain, second_chain = hop(first_chain), hop(second_chain)
        state = step(arrived, distance, state)
    arrived, state = after(first_chain, state)
    halves = [hop(arrived[:2]), hop(arrived[2:])]
    state = step([arrived], 3, state)
    second_chain, state = after(second_chain, state)
    state = step([second_chain], 3, state, chains=(1,))
    block, state = after(halves[0], state)
    state = step([block], 4, state)
    with jax.named_scope("swap_terms"):
        early = swap(state[:2, :, ROWS:])
    block, state = after(halves[1], state)
    late = step([block], 4, state, 1, begin=2, steps=(2, 3))
    with jax.named_scope("swap_terms"):
        late = swap(late)
    mine = step([block], 4, state, 0, begin=2, steps=(2, 3))
    with jax.named_scope("join"):
        attended = call(
            join,
            jax.ShapeDtypeStruct((heads, SLICE, HD), bf16),
            [smem, vmem, vmem, vmem, vmem],
        )(lengths, state, mine, early, late)
    with jax.named_scope("heads_to_tokens"):
        attended = lax.all_to_all(attended, ("y", "x"), 0, 0, tiled=True)
    with jax.named_scope("unpack"):
        out = call(unpack, jax.ShapeDtypeStruct((SLICE, heads * HD), bf16), [vmem])(attended)
    return out[None]


def solution(mesh):
    fine = Mesh(mesh.devices.reshape(2, 4, 2, 4, 4), ("zlo", "y", "core", "x", "zhi"))
    span, seq = ("zlo", "y", "core"), ("x", "zhi")
    return jax.shard_map(
        shards,
        mesh=fine,
        in_specs=(P(None, span, seq, None), P()),
        out_specs=P(span, seq, None),
        check_vma=False,
    )
```

```python
import functools
import math

import jax
import jax.numpy as jnp
from jax import lax
from jax.experimental import pallas as pl
from jax.experimental.pallas import tpu as pltpu
from jax.sharding import Mesh
from jax.sharding import PartitionSpec as P

HD = 128
SLICE = 64
ROWS = 256
FILL = -1e30
STATE = HD + 16
SCALE = math.log2(math.e) / math.sqrt(HD)
VMEM = pltpu.VMEM
RING = ("zlo", "core", "zhi")


def pack(qkv_ref, out_ref):
    for head in range(out_ref.shape[0]):
        columns = slice(head * HD, (head + 1) * HD)
        for part in range(3):
            out_ref[head, part * SLICE : (part + 1) * SLICE] = qkv_ref[part, :, columns]


def unpack(parts_ref, out_ref):
    for head in range(parts_ref.shape[0]):
        out_ref[:, head * HD : (head + 1) * HD] = parts_ref[head]


def split(parts_ref, query_ref, pair_ref):
    for span in range(4):
        block = parts_ref.at[4 * span : 4 * span + 4]
        query_ref[span] = block[:, :SLICE, :].reshape(ROWS, HD)
        pair_ref[span, :ROWS] = block[:, SLICE : 2 * SLICE, :].reshape(ROWS, HD)
        turned = block[:, 2 * SLICE :, :].reshape(ROWS, HD).T
        pair_ref[span, ROWS : ROWS + HD] = turned[:, :HD]
        pair_ref[span, ROWS + HD :] = turned[:, HD:]


def attend(distance, first, half, *refs):
    refs = list(refs)
    lengths_ref, own_ref, other_ref = refs[:3]
    arrivals = refs[3:-1] if first else refs[3:-2]
    before_ref = None if first else refs[-2]
    state_ref = refs[-1]
    core = lax.axis_index("core")
    zlo = lax.axis_index("zlo")
    zed = lax.axis_index("zhi") * 2 + zlo
    pieces = [(span, number) for span in range(4) for number in range(len(arrivals))]
    source_zed = lax.rem(zed + 8 + jnp.where(core == 0, -distance, distance), 8)
    source_zlo = lax.rem(source_zed, 2)
    source_core = [core, 1 - core]
    offset = (source_zed // 2) * SLICE
    aligned = distance % 2 == 0

    width = state_ref.shape[2]
    columns = slice(ROWS if half == 1 else 0, ROWS if half == 0 else 2 * ROWS)

    ones = jnp.where(lax.broadcasted_iota(jnp.int32, (16, ROWS), 0) < 8, 1.0, 0.0)
    ones = ones.astype(jnp.bfloat16)

    def scores_of(step, count, last):
        if half is None:
            queries = jnp.concatenate([own_ref[step], other_ref[step]], axis=0)
        else:
            queries = (own_ref, other_ref)[half][step]
        row = lax.broadcasted_iota(jnp.int32, (SLICE, width), 0)
        other_half = lax.broadcasted_iota(jnp.int32, (SLICE, width), 1) >= ROWS
        scores = []
        for span, number in pieces:
            if span >= count:
                continue
            score = lax.dot_general(
                arrivals[number][span, :ROWS, :],
                queries,
                (((1,), (1,)), ((), ())),
                preferred_element_type=jnp.float32,
            )
            live = lengths_ref[source_zlo * 8 + 2 * span + source_core[number]]
            for part in range(4):
                rows = score[part * SLICE : (part + 1) * SLICE]
                bound = live - part * ROWS - offset
                if span == last:
                    own_bound = jnp.where(source_core[number] <= core, bound, 0)
                    other_bound = jnp.where(source_core[number] <= 1 - core, bound, 0)
                    if half is None:
                        bound = jnp.where(other_half, other_bound, own_bound)
                    else:
                        bound = (own_bound, other_bound)[half]
                    rows = jnp.where(row < bound, rows, FILL)
                elif part >= 2:
                    rows = jnp.where(row < bound, rows, FILL)
                scores.append(rows)
        return jnp.concatenate(scores, axis=0)

    def values_of(count):
        values = []
        for span, number in pieces:
            if span < count:
                block = arrivals[number].at[span]
                turned = jnp.concatenate([block[ROWS : ROWS + HD, :], block[ROWS + HD :, :]], axis=1)
                values.append(jnp.concatenate([turned, ones], axis=0))
        return jnp.concatenate(values, axis=1)

    def add(steps):
        scores = [scores_of(*step) for step in steps]
        olds = [None if first else before_ref[step, HD + 8 : HD + 9, columns] for step, _, _ in steps]
        peaks = []
        for old, score in zip(olds, scores):
            peak = jnp.max(score, axis=0, keepdims=True)
            peaks.append(peak if first else jnp.maximum(old, peak))
        weights = []
        for (_, _, last), score, peak in zip(steps, scores, peaks):
            weight = jnp.exp2((score - peak) * SCALE)
            if last == 0:
                weight = jnp.where(score > FILL, weight, 0.0)
            weights.append(weight.astype(jnp.bfloat16))
        fresh = [
            jnp.dot(values_of(count), weight, preferred_element_type=jnp.float32)[: HD + 8]
            for (_, count, _), weight in zip(steps, weights)
        ]
        for (step, _, _), old, peak, term in zip(steps, olds, peaks, fresh):
            if not first:
                keep = jnp.exp2((old - peak) * SCALE)
                term = before_ref[step, : HD + 8, columns] * keep + term
            state_ref[step, : HD + 8, :] = term
            state_ref[step, HD + 8 :, :] = jnp.broadcast_to(peak, (8, width))

    if aligned:
        add([(step, step + 1, step) for step in range(4)])
    else:

        @pl.when(source_zlo < zlo)
        def _():
            @pl.loop(0, 2)
            def _(pair):
                add([(2 * pair, 4, -1), (2 * pair + 1, 4, -1)])

        @pl.when(source_zlo > zlo)
        def _():
            state_ref[...] = before_ref[...]


def join(lengths_ref, own_ref, other_ref, out_ref):
    core = lax.axis_index("core")
    zlo = lax.axis_index("zlo")
    offset = lax.axis_index("zhi") * SLICE
    for step in range(4):
        live = lengths_ref[zlo * 8 + 2 * step + core]
        first_peak = own_ref[step, HD + 8 : HD + 9, :]
        second_peak = other_ref[step, HD + 8 : HD + 9, :]
        peak = jnp.maximum(first_peak, second_peak)
        first = jnp.exp2((first_peak - peak) * SCALE)
        second = jnp.exp2((second_peak - peak) * SCALE)
        total = own_ref[step, HD : HD + 1, :] * first + other_ref[step, HD : HD + 1, :] * second
        numerator = own_ref[step, :HD, :] * first + other_ref[step, :HD, :] * second
        result = (numerator / total).T
        row = lax.broadcasted_iota(jnp.int32, (SLICE, HD), 0)
        for piece in range(4):
            part = result[piece * SLICE : (piece + 1) * SLICE]
            part = jnp.where(row < live - piece * ROWS - offset, part, 0.0)
            out_ref[4 * step + piece] = part.astype(jnp.bfloat16)


def call(kernel, out_shape, in_specs, flops=0, moved=0, **kw):
    spec = pl.BlockSpec(memory_space=VMEM)
    return pl.pallas_call(
        kernel,
        out_shape=out_shape,
        in_specs=in_specs,
        out_specs=jax.tree.map(lambda _: spec, out_shape),
        compiler_params=pltpu.CompilerParams(vmem_limit_bytes=40 * 2**20),
        cost_estimate=pl.CostEstimate(flops=flops, bytes_accessed=moved, transcendentals=0),
        **kw,
    )


def shards(qkv, lengths):
    vmem = pl.BlockSpec(memory_space=VMEM)
    smem = pl.BlockSpec(memory_space=pltpu.SMEM)
    heads = 16
    bf16 = jnp.bfloat16
    with jax.named_scope("pack"):
        parts = call(pack, jax.ShapeDtypeStruct((heads, 3 * SLICE, HD), bf16), [vmem])(qkv[:, 0])
    with jax.named_scope("tokens_to_heads"):
        parts = lax.all_to_all(parts, ("y", "x"), 0, 0, tiled=True)
    chips = 8
    place = [z % 2 * 8 + z // 2 for z in range(chips)]
    route = [(place[z], place[(z + 1) % chips]) for z in range(chips)]
    route += [(place[z] + 4, place[(z - 1) % chips] + 4) for z in range(chips)]

    def hop(block):
        with jax.named_scope("ring"):
            return lax.ppermute(block, RING, route)

    def swap(block):
        return lax.ppermute(block, "core", [(0, 1), (1, 0)])

    def divide(parts):
        with jax.named_scope("split"):
            return call(
                split,
                [
                    jax.ShapeDtypeStruct((4, ROWS, HD), bf16),
                    jax.ShapeDtypeStruct((4, 2 * ROWS, HD), bf16),
                ],
                [vmem],
            )(parts)

    with jax.named_scope("swap_parts"):
        other_parts = swap(parts)
    own, pairs = divide(parts)
    first_chain = hop(pairs)
    other, second = divide(other_parts)
    second_chain = hop(second)

    def step(arrivals, distance, state, half=None):
        first = state is None
        operands = [lengths, own, other] + arrivals + ([] if first else [state])
        count = 4 * len(arrivals)
        width = 2 * ROWS if half is None else ROWS
        with jax.named_scope("attend"):
            return call(
                functools.partial(attend, distance, first, half),
                jax.ShapeDtypeStruct((4, STATE, width), jnp.float32),
                [smem] + [vmem] * (len(operands) - 1),
                flops=16 * HD * ROWS * width * 4 * count,
                moved=8 * 2**20,
                input_output_aliases={} if first or half is not None else {len(operands) - 1: 0},
            )(*operands)

    state = step([pairs], 0, None)
    for distance in range(1, 4):
        first_chain, state = lax.optimization_barrier((first_chain, state))
        second_chain, state = lax.optimization_barrier((second_chain, state))
        arrived = [first_chain, second_chain]
        first_chain = hop(first_chain)
        if distance < 3:
            second_chain = hop(second_chain)
        state = step(arrived, distance, state)
    theirs = step([first_chain], 4, state, 1)
    with jax.named_scope("swap_terms"):
        theirs = swap(theirs)
    mine = step([first_chain], 4, state, 0)
    with jax.named_scope("join"):
        attended = call(
            join,
            jax.ShapeDtypeStruct((heads, SLICE, HD), bf16),
            [smem, vmem, vmem],
        )(lengths, mine, theirs)
    with jax.named_scope("heads_to_tokens"):
        attended = lax.all_to_all(attended, ("y", "x"), 0, 0, tiled=True)
    with jax.named_scope("unpack"):
        out = call(unpack, jax.ShapeDtypeStruct((SLICE, heads * HD), bf16), [vmem])(attended)
    return out[None]


def solution(mesh):
    fine = Mesh(mesh.devices.reshape(2, 4, 2, 4, 4), ("zlo", "y", "core", "x", "zhi"))
    span, seq = ("zlo", "y", "core"), ("x", "zhi")
    return jax.shard_map(
        shards,
        mesh=fine,
        in_specs=(P(None, span, seq, None), P()),
        out_specs=P(span, seq, None),
        check_vma=False,
    )
```

```python
import functools
import math

import jax
import jax.numpy as jnp
from jax import lax
from jax.experimental import pallas as pl
from jax.experimental.pallas import tpu as pltpu
from jax.sharding import Mesh
from jax.sharding import PartitionSpec as P

HD = 128
SLICE = 64
ROWS = 256
FILL = -1e30
STATE = HD + 16
SCALE = math.log2(math.e) / math.sqrt(HD)
VMEM = pltpu.VMEM
RING = ("zlo", "core", "zhi")


def pack(qkv_ref, out_ref):
    for head in range(out_ref.shape[0]):
        columns = slice(head * HD, (head + 1) * HD)
        for part in range(3):
            out_ref[head, part * SLICE : (part + 1) * SLICE] = qkv_ref[part, :, columns]


def unpack(parts_ref, out_ref):
    for head in range(parts_ref.shape[0]):
        out_ref[:, head * HD : (head + 1) * HD] = parts_ref[head]


def split(parts_ref, query_ref, pair_ref):
    for span in range(4):
        block = parts_ref.at[4 * span : 4 * span + 4]
        query_ref[span] = block[:, :SLICE, :].reshape(ROWS, HD)
        pair_ref[span, :ROWS] = block[:, SLICE : 2 * SLICE, :].reshape(ROWS, HD)
        turned = block[:, 2 * SLICE :, :].reshape(ROWS, HD).T
        pair_ref[span, ROWS : ROWS + HD] = turned[:, :HD]
        pair_ref[span, ROWS + HD :] = turned[:, HD:]


def attend(distance, chains, first, half, *refs):
    refs = list(refs)
    lengths_ref, own_ref, other_ref = refs[:3]
    arrivals = refs[3:-1] if first else refs[3:-2]
    before_ref = None if first else refs[-2]
    state_ref = refs[-1]
    core = lax.axis_index("core")
    zlo = lax.axis_index("zlo")
    zed = lax.axis_index("zhi") * 2 + zlo
    pieces = [(span, number) for span in range(4) for number in range(len(arrivals))]
    source_zed = lax.rem(zed + 8 + jnp.where(core == 0, -distance, distance), 8)
    source_zlo = lax.rem(source_zed, 2)
    source_core = [core if chain == 0 else 1 - core for chain in chains]
    offset = (source_zed // 2) * SLICE
    aligned = distance % 2 == 0

    width = state_ref.shape[2]
    columns = slice(ROWS if half == 1 else 0, ROWS if half == 0 else 2 * ROWS)

    ones = jnp.where(lax.broadcasted_iota(jnp.int32, (16, ROWS), 0) < 8, 1.0, 0.0)
    ones = ones.astype(jnp.bfloat16)

    def scores_of(step, count, last):
        if half is None:
            queries = jnp.concatenate([own_ref[step], other_ref[step]], axis=0)
        else:
            queries = (own_ref, other_ref)[half][step]
        row = lax.broadcasted_iota(jnp.int32, (SLICE, width), 0)
        other_half = lax.broadcasted_iota(jnp.int32, (SLICE, width), 1) >= ROWS
        scores = []
        for span, number in pieces:
            if span >= count:
                continue
            score = lax.dot_general(
                arrivals[number][span, :ROWS, :],
                queries,
                (((1,), (1,)), ((), ())),
                preferred_element_type=jnp.float32,
            )
            live = lengths_ref[source_zlo * 8 + 2 * span + source_core[number]]
            for part in range(4):
                rows = score[part * SLICE : (part + 1) * SLICE]
                bound = live - part * ROWS - offset
                if span == last:
                    own_bound = jnp.where(source_core[number] <= core, bound, 0)
                    other_bound = jnp.where(source_core[number] <= 1 - core, bound, 0)
                    if half is None:
                        bound = jnp.where(other_half, other_bound, own_bound)
                    else:
                        bound = (own_bound, other_bound)[half]
                    rows = jnp.where(row < bound, rows, FILL)
                elif part >= 2:
                    rows = jnp.where(row < bound, rows, FILL)
                scores.append(rows)
        return jnp.concatenate(scores, axis=0)

    def values_of(count):
        values = []
        for span, number in pieces:
            if span < count:
                block = arrivals[number].at[span]
                turned = jnp.concatenate([block[ROWS : ROWS + HD, :], block[ROWS + HD :, :]], axis=1)
                values.append(jnp.concatenate([turned, ones], axis=0))
        return jnp.concatenate(values, axis=1)

    def add(steps):
        scores = [scores_of(*step) for step in steps]
        olds = [None if first else before_ref[step, HD + 8 : HD + 9, columns] for step, _, _ in steps]
        peaks = []
        for old, score in zip(olds, scores):
            peak = jnp.max(score, axis=0, keepdims=True)
            peaks.append(peak if first else jnp.maximum(old, peak))
        weights = []
        for (_, _, last), score, peak in zip(steps, scores, peaks):
            weight = jnp.exp2((score - peak) * SCALE)
            if last == 0:
                weight = jnp.where(score > FILL, weight, 0.0)
            weights.append(weight.astype(jnp.bfloat16))
        fresh = [
            jnp.dot(values_of(count), weight, preferred_element_type=jnp.float32)[: HD + 8]
            for (_, count, _), weight in zip(steps, weights)
        ]
        for (step, _, _), old, peak, term in zip(steps, olds, peaks, fresh):
            if not first:
                keep = jnp.exp2((old - peak) * SCALE)
                term = before_ref[step, : HD + 8, columns] * keep + term
            state_ref[step, : HD + 8, :] = term
            state_ref[step, HD + 8 :, :] = jnp.broadcast_to(peak, (8, width))

    if aligned:
        add([(step, step + 1, step) for step in range(4)])
    else:

        @pl.when(source_zlo < zlo)
        def _():
            together = 4 // len(arrivals)

            @pl.loop(0, len(arrivals))
            def _(group):
                add([(together * group + member, 4, -1) for member in range(together)])

        @pl.when(source_zlo > zlo)
        def _():
            state_ref[...] = before_ref[...]


def join(lengths_ref, own_ref, other_ref, out_ref):
    core = lax.axis_index("core")
    zlo = lax.axis_index("zlo")
    offset = lax.axis_index("zhi") * SLICE
    for step in range(4):
        live = lengths_ref[zlo * 8 + 2 * step + core]
        first_peak = own_ref[step, HD + 8 : HD + 9, :]
        second_peak = other_ref[step, HD + 8 : HD + 9, :]
        peak = jnp.maximum(first_peak, second_peak)
        first = jnp.exp2((first_peak - peak) * SCALE)
        second = jnp.exp2((second_peak - peak) * SCALE)
        total = own_ref[step, HD : HD + 1, :] * first + other_ref[step, HD : HD + 1, :] * second
        numerator = own_ref[step, :HD, :] * first + other_ref[step, :HD, :] * second
        result = (numerator / total).T
        row = lax.broadcasted_iota(jnp.int32, (SLICE, HD), 0)
        for piece in range(4):
            part = result[piece * SLICE : (piece + 1) * SLICE]
            part = jnp.where(row < live - piece * ROWS - offset, part, 0.0)
            out_ref[4 * step + piece] = part.astype(jnp.bfloat16)


def call(kernel, out_shape, in_specs, flops=0, moved=0, **kw):
    spec = pl.BlockSpec(memory_space=VMEM)
    return pl.pallas_call(
        kernel,
        out_shape=out_shape,
        in_specs=in_specs,
        out_specs=jax.tree.map(lambda _: spec, out_shape),
        compiler_params=pltpu.CompilerParams(vmem_limit_bytes=40 * 2**20),
        cost_estimate=pl.CostEstimate(flops=flops, bytes_accessed=moved, transcendentals=0),
        **kw,
    )


def shards(qkv, lengths):
    vmem = pl.BlockSpec(memory_space=VMEM)
    smem = pl.BlockSpec(memory_space=pltpu.SMEM)
    heads = 16
    bf16 = jnp.bfloat16
    with jax.named_scope("pack"):
        parts = call(pack, jax.ShapeDtypeStruct((heads, 3 * SLICE, HD), bf16), [vmem])(qkv[:, 0])
    with jax.named_scope("tokens_to_heads"):
        parts = lax.all_to_all(parts, ("y", "x"), 0, 0, tiled=True)
    chips = 8
    place = [z % 2 * 8 + z // 2 for z in range(chips)]
    route = [(place[z], place[(z + 1) % chips]) for z in range(chips)]
    route += [(place[z] + 4, place[(z - 1) % chips] + 4) for z in range(chips)]

    def hop(block):
        with jax.named_scope("ring"):
            return lax.ppermute(block, RING, route)

    def swap(block):
        return lax.ppermute(block, "core", [(0, 1), (1, 0)])

    def divide(parts):
        with jax.named_scope("split"):
            return call(
                split,
                [
                    jax.ShapeDtypeStruct((4, ROWS, HD), bf16),
                    jax.ShapeDtypeStruct((4, 2 * ROWS, HD), bf16),
                ],
                [vmem],
            )(parts)

    with jax.named_scope("swap_parts"):
        other_parts = swap(parts)
    own, pairs = divide(parts)
    first_chain = hop(pairs)
    other, second = divide(other_parts)
    second_chain = hop(second)

    def step(arrivals, distance, state, half=None, chains=(0, 1)):
        first = state is None
        operands = [lengths, own, other] + arrivals + ([] if first else [state])
        count = 4 * len(arrivals)
        width = 2 * ROWS if half is None else ROWS
        with jax.named_scope("attend"):
            return call(
                functools.partial(attend, distance, chains[: len(arrivals)], first, half),
                jax.ShapeDtypeStruct((4, STATE, width), jnp.float32),
                [smem] + [vmem] * (len(operands) - 1),
                flops=16 * HD * ROWS * width * 4 * count,
                moved=8 * 2**20,
                input_output_aliases={} if first or half is not None else {len(operands) - 1: 0},
            )(*operands)

    state = step([pairs], 0, None)
    def after(block, state):
        return lax.optimization_barrier((block, state))

    for distance in range(1, 3):
        first_chain, state = after(first_chain, state)
        second_chain, state = after(second_chain, state)
        arrived = [first_chain, second_chain]
        first_chain, second_chain = hop(first_chain), hop(second_chain)
        state = step(arrived, distance, state)
    arrived, state = after(first_chain, state)
    first_chain = hop(arrived)
    state = step([arrived], 3, state)
    second_chain, state = after(second_chain, state)
    state = step([second_chain], 3, state, chains=(1,))
    theirs = step([first_chain], 4, state, 1)
    with jax.named_scope("swap_terms"):
        theirs = swap(theirs)
    mine = step([first_chain], 4, state, 0)
    with jax.named_scope("join"):
        attended = call(
            join,
            jax.ShapeDtypeStruct((heads, SLICE, HD), bf16),
            [smem, vmem, vmem],
        )(lengths, mine, theirs)
    with jax.named_scope("heads_to_tokens"):
        attended = lax.all_to_all(attended, ("y", "x"), 0, 0, tiled=True)
    with jax.named_scope("unpack"):
        out = call(unpack, jax.ShapeDtypeStruct((SLICE, heads * HD), bf16), [vmem])(attended)
    return out[None]


def solution(mesh):
    fine = Mesh(mesh.devices.reshape(2, 4, 2, 4, 4), ("zlo", "y", "core", "x", "zhi"))
    span, seq = ("zlo", "y", "core"), ("x", "zhi")
    return jax.shard_map(
        shards,
        mesh=fine,
        in_specs=(P(None, span, seq, None), P()),
        out_specs=P(span, seq, None),
        check_vma=False,
    )
```
